128 devices in a mesh: dp: 16 (over x_hi, y, core), tensor: 8 (over x_lo, z).
Axes of the slice: x: 4 (x_hi: 2, x_lo: 2; x = x_hi * 2 + x_lo), y: 4, z: 4, core: 2. Of those that a mesh axis runs over, the one named last changes fastest.
Arguments:
- teacher_hidden: bfloat16 [2048, 4096], P('dp'), may hold values from -6 to 6
- student_hidden: bfloat16 [2048, 2048], P('dp'), may hold values from -6 to 6
- target_ids: int32 [2048], P('dp'), may hold values from 0 to 64127
- teacher_head: bfloat16 [4096, 65536], P(None, ('dp', 'tensor')), may hold values from -1 to 1
- student_head: bfloat16 [2048, 65536], P(None, ('dp', 'tensor')), may hold values from -1 to 1
Outputs:
- head_grad: float32 [2048, 65536], P(None, ('dp', 'tensor'))
- input_grad: float32 [2048, 2048], P('dp', 'tensor')
The draws below stay inside these ranges and needn't reach their ends.
All inputs are finite; a program needn't handle non-finite values.
Results may differ from the reference program's by a relative error of at most 0.0065.
Values may be sent and summed in bfloat16 or wider, within the bound.
No kernel may reach another device: no remote copies, remote signals or barrier semaphores. Data moves between devices by JAX's collectives and lax.ppermute only.
A program may use at most 128 MiB of HBM per device.

```python
import math
import jax
import jax.numpy as jnp
import numpy as np
from jax import lax

DT = 4096
DS = 2048
VOCAB = 64128
PADDED = 65536
TOKENS = 2048


def column_vectors(head_key, depth, indices):
    scale = 4.0 / jnp.sqrt(jnp.float32(depth))
    one_column = lambda index: jax.random.normal(jax.random.fold_in(head_key, index), (depth,), jnp.float32)
    return jax.vmap(one_column)(indices) * scale


def head_matrix(key, salt, depth):
    head_key = jax.random.fold_in(key, salt)
    columns = column_vectors(head_key, depth, jnp.arange(PADDED, dtype=jnp.int32))
    return jnp.clip(columns.T, -1.0, 1.0).astype(jnp.bfloat16)


def hidden_rows(key, salt, depth):
    drawn_rows = jnp.clip(jax.random.normal(jax.random.fold_in(key, salt), (TOKENS, depth), jnp.float32), -6.0, 6.0)
    return drawn_rows.astype(jnp.bfloat16)


def draw_teacher_head(key, part):
    return head_matrix(key, 101, DT)


def draw_student_head(key, part):
    return head_matrix(key, 202, DS)


def draw_teacher_hidden(key, part):
    return hidden_rows(key, 303, DT)


def draw_student_hidden(key, part):
    return hidden_rows(key, 404, DS)


def plant(drawn, own_key, least, top_value):
    longest = drawn.shape.index(max(drawn.shape))
    spots = []
    for shift in (0, 1):
        where = [jax.random.randint(jax.random.fold_in(own_key, axis), (), 0, length) for axis, length in enumerate(drawn.shape)]
        where[longest] = (where[longest] + shift) % drawn.shape[longest]
        spots.append(tuple(where))
    return drawn.at[spots[0]].set(least).at[spots[1]].set(top_value)


def rank_table(number_of, slope):
    portions = [(1 << 20) // math.isqrt(standing ** slope) + 1 for standing in range(1, number_of + 1)]
    scale = 1 + sum(portions) // (1 << 30)
    return np.cumsum(np.array([max(1, weight // scale) for weight in portions]))


def ranked_ids(stream_key, extent, count, slope):
    table = rank_table(count, slope)
    pick = jax.random.randint(jax.random.fold_in(stream_key, 1), extent, 0, int(table[count - 1]))
    rank = jnp.searchsorted(jnp.asarray(table, jnp.int32), pick, side="right")
    return jax.random.permutation(jax.random.fold_in(stream_key, 2), count)[rank].astype(jnp.int32)


def setup_inputs(seed: int = 0) -> dict:
    streams_of = jax.random.split(jax.random.key(seed), 6)
    teacher_hidden = draw_teacher_hidden(jax.random.fold_in(streams_of[5], 71), 0)
    student_hidden = draw_student_hidden(jax.random.fold_in(streams_of[5], 71), 0)
    target_ids = plant(ranked_ids(streams_of[2], (TOKENS,), VOCAB, 2), jax.random.fold_in(streams_of[2], 3), 0, VOCAB - 1).astype(jnp.int32)
    teacher_head = draw_teacher_head(jax.random.fold_in(streams_of[5], 71), 0)
    student_head = draw_student_head(jax.random.fold_in(streams_of[5], 71), 0)
    return {"teacher_hidden": teacher_hidden, "student_hidden": student_hidden, "target_ids": target_ids, "teacher_head": teacher_head, "student_head": student_head}


def softmax_rows(logits):
    peak = jnp.max(logits, axis=1, keepdims=True)
    expo = jnp.exp(logits - peak)
    return expo / jnp.sum(expo, axis=1, keepdims=True)


def reference(teacher_hidden, student_hidden, target_ids, teacher_head, student_head):
    columns = jnp.arange(PADDED, dtype=jnp.int32)
    is_real = (columns < VOCAB)[None, :]
    teacher_logits = jnp.where(is_real, jnp.dot(teacher_hidden, teacher_head, preferred_element_type=jnp.float32), jnp.float32(-1e30))
    student_logits = jnp.where(is_real, jnp.dot(student_hidden, student_head, preferred_element_type=jnp.float32), jnp.float32(-1e30))
    teacher_probs = softmax_rows(teacher_logits)
    student_probs = softmax_rows(student_logits)
    onehot = (target_ids[:, None] == columns[None, :]).astype(jnp.float32)
    logit_grad = (2.0 * student_probs - teacher_probs - onehot).astype(jnp.bfloat16)
    head_grad = lax.dot_general(student_hidden, logit_grad, (((0,), (0,)), ((), ())), preferred_element_type=jnp.float32)
    input_grad = lax.dot_general(logit_grad, student_head, (((1,), (1,)), ((), ())), preferred_element_type=jnp.float32)
    return head_grad, input_grad
```

```python
import jax
import jax.numpy as jnp
from jax import lax
from jax.sharding import PartitionSpec as P

VOCAB = 64128
F32, BF16 = jnp.float32, jnp.bfloat16
AXES = ("dp", "tensor")

BLOCK_DIMS = ("X1", "Ya", "Yb")
SLICE_DIMS = ("X0", "Zb", "Za")
PARTS = (
    (0, 8, ("Zb", "Za"), ("X1", "Ya", "Yb", "Za", "Zb")),
    (32, 8, ("Zb", "Za"), ("Ya", "X1", "Yb", "Zb", "Za")),
    (64, 16, ("X0",), ("Yb", "Ya", "X0", "X1")),
    (96, 32, (), ("X1", "Yb", "Ya")),
)
STAT_ORDER = ("Ya", "Za", "X0", "X1", "Zb", "Yb")
REDUCE_GROUPS = (((0, 1), ("Zb", "Yb", "Za", "Ya", "X1", "X0")), ((2, 3), ("Yb", "Zb", "Ya", "Za", "X1", "X0")))
NARROW_STEPS = 3


def bits_of(dev):
    dp, tensor = dev // 8, dev % 8
    xh, y, core = dp // 8, (dp // 2) % 4, dp % 2
    xl, z = tensor // 4, tensor % 4
    gy, gz = y ^ (y // 2), z ^ (z // 2)
    pick = lambda g, second: (g // 2) * second + (g % 2) * (1 - second)
    return {
        "X1": xh, "X0": xh ^ xl,
        "Ya": pick(gy, core), "Yb": pick(gy, 1 - core),
        "Za": pick(gz, core), "Zb": pick(gz, 1 - core),
        "C": core,
    }


def z_of(bits):
    core = bits["C"]
    high = bits["Zb"] * (1 - core) + bits["Za"] * core
    low = bits["Za"] * (1 - core) + bits["Zb"] * core
    return high * 2 + (high ^ low)


def pairs(dim):
    key = lambda b: tuple(sorted(b.items()))
    table = {key(bits_of(d)): d for d in range(128)}
    partner = lambda b: dict(b, **{dim: 1 - b[dim]})
    if dim == "C":
        return [(d, d ^ 8) for d in range(128)]
    return [(d, table[key(partner(bits_of(d)))]) for d in range(128)]


def swap(x, dim):
    return lax.ppermute(x, AXES, pairs(dim))


def split(x, axis, pre):
    shape = x.shape
    n = shape[axis]
    y = x.reshape(shape[:axis] + (pre, 2, n // (2 * pre)) + shape[axis + 1 :])
    out = shape[:axis] + (n // 2,) + shape[axis + 1 :]
    return [lax.index_in_dim(y, i, axis + 1, keepdims=False).reshape(out) for i in (0, 1)]


def flip(x, axis, pre):
    shape = x.shape
    n = shape[axis]
    y = x.reshape(shape[:axis] + (pre, 2, n // (2 * pre)) + shape[axis + 1 :])
    y = jnp.concatenate([lax.slice_in_dim(y, 1, 2, axis=axis + 1), lax.slice_in_dim(y, 0, 1, axis=axis + 1)], axis + 1)
    return y.reshape(shape)


def body(teacher_hidden, student_hidden, target_ids, teacher_head, student_head):
    dev = lax.axis_index("dp") * 8 + lax.axis_index("tensor")
    bit = bits_of(dev)
    width = teacher_head.shape[1]
    dt, ds = teacher_hidden.shape[1], student_hidden.shape[1]

    ids = jnp.stack([target_ids // 256, target_ids % 256], axis=1).astype(BF16)
    own = jnp.concatenate([teacher_hidden, student_hidden, jnp.pad(ids, ((0, 0), (0, 126)))], axis=1)

    chunks, axes_of = [], []
    for first, n, slices, order in PARTS:
        index = 0
        for d in slices:
            index = index * 2 + bit[d]
        x = lax.dynamic_slice_in_dim(own, first + index * n, n, 0) if slices else own[first : first + n]
        for d in order[:-1]:
            x = jnp.concatenate([x, swap(x, d)], axis=0)
        chunks.append([x, swap(x, order[-1])])
        axes_of.append(list(order[::-1]))

    head_t = jnp.concatenate([teacher_head, swap(teacher_head, "C")], axis=1)
    head_s = jnp.concatenate([student_head, swap(student_head, "C")], axis=1)
    lane = lax.iota(jnp.int32, 2 * width)
    columns = jnp.where(lane < width, dev * width + lane, (dev ^ 8) * width + lane - width)
    is_real = (columns < VOCAB)[None, :]

    wide = ds // 8
    blocks = []
    for x0 in (0, 1):
        for zb in (0, 1):
            for za in (0, 1):
                xl = bit["X0"] ^ x0 ^ bit["X1"]
                z = z_of({"C": bit["C"], "Zb": bit["Zb"] ^ zb, "Za": bit["Za"] ^ za})
                blocks.append(lax.dynamic_slice_in_dim(head_s, (xl * 4 + z) * wide, wide, 0))
    head_r = jnp.concatenate(blocks, axis=0)

    logits, stats = [], []
    for chunk in chunks:
        tops, sums = [], []
        for x in chunk:
            z_t = jnp.dot(x[:, :dt], head_t, preferred_element_type=F32)
            z_s = jnp.dot(x[:, dt : dt + ds], head_s, preferred_element_type=F32)
            z_t, z_s = (jnp.where(is_real, z, F32(-1e30)) for z in (z_t, z_s))
            m_t, m_s = jnp.max(z_t, axis=1), jnp.max(z_s, axis=1)
            tops.append(jnp.stack([m_t, m_s]))
            sums.append(
                jnp.stack([
                    jnp.sum(jnp.exp(z_t - m_t[:, None]), axis=1),
                    jnp.sum(jnp.exp(z_s - m_s[:, None]), axis=1),
                ])
            )
            logits.append((z_t, z_s))
        stats.append((jnp.concatenate(tops, axis=1), jnp.concatenate(sums, axis=1)))

    size = [t.shape[1] for t, _ in stats]
    edge = [sum(size[:i]) for i in range(len(size) + 1)]
    both = jnp.concatenate([jnp.concatenate([t for t, _ in stats], axis=1), jnp.concatenate([s for _, s in stats], axis=1)], axis=0)
    for d in STAT_ORDER:
        other = swap(both, d)
        pieces = []
        for i, axes in enumerate(axes_of):
            piece = other[:, edge[i] : edge[i + 1]]
            pieces.append(flip(piece, 1, 1 << axes.index(d)) if d in axes else piece)
        other = jnp.concatenate(pieces, axis=1)
        top = jnp.maximum(both[:2], other[:2])
        both = jnp.concatenate(
            [top, both[2:] * jnp.exp(both[:2] - top) + other[2:] * jnp.exp(other[:2] - top)], axis=0
        )

    grads, rows, terms = [], [], []
    at = 0
    for i, chunk in enumerate(chunks):
        mine = []
        for x in chunk:
            z_t, z_s = logits[len(grads)]
            n = x.shape[0]
            peak_t, peak_s, sum_t, sum_s = (both[j, at : at + n][:, None] for j in range(4))
            digits = x[:, dt + ds : dt + ds + 2].astype(jnp.int32)
            onehot = (digits[:, :1] * 256 + digits[:, 1:2] == columns[None, :]).astype(F32)
            p_t = jnp.exp(z_t - peak_t) / sum_t
            p_s = jnp.exp(z_s - peak_s) / sum_s
            g = (2.0 * p_s - p_t - onehot).astype(BF16)
            grads.append(g)
            mine.append(g)
            rows.append(x[:, dt : dt + ds])
            at += n
        terms.append(
            lax.dot_general(
                jnp.concatenate(mine, axis=0), head_r, (((1,), (1,)), ((), ())), preferred_element_type=F32
            )
        )

    result = [None] * len(PARTS)
    for members, order in REDUCE_GROUPS:
        arrays = {i: terms[i] for i in members}
        axes = {i: list(axes_of[i]) for i in members}
        cols = list(SLICE_DIMS)
        for step, d in enumerate(order):
            keep, send = {}, []
            for i in members:
                if d in BLOCK_DIMS:
                    halves = split(arrays[i], 0, 1 << axes[i].index(d))
                else:
                    halves = split(arrays[i], 1, 1 << cols.index(d))
                keep[i] = halves[0]
                send.append(halves[1])
            out = jnp.concatenate(send, axis=0)
            back = swap(out.astype(BF16) if step < NARROW_STEPS else out, d).astype(F32)
            start = 0
            for i in members:
                if d in BLOCK_DIMS:
                    axes[i].remove(d)
                n = keep[i].shape[0]
                got = back[start : start + n]
                start += n
                if d in axes[i]:
                    got = flip(got, 0, 1 << axes[i].index(d))
                if d == "X1":
                    got = flip(got, 1, 1 << cols.index("X0"))
                arrays[i] = keep[i] + got
            if d in cols:
                cols.remove(d)
        for i in members:
            first, n, slices, _ = PARTS[i]
            x = arrays[i]
            pieces = []
            for s in range(x.shape[0] // n):
                index = 0
                for d in axes[i]:
                    where = (s >> (len(slices) - 1 - slices.index(d))) & 1
                    index = index * 2 + (where ^ bit[d])
                pieces.append(lax.dynamic_slice_in_dim(x, index * n, n, 0) if slices else x)
            result[i] = jnp.concatenate(pieces, axis=0)
    input_grad = jnp.concatenate(result, axis=0)

    all_rows, all_grads = jnp.concatenate(rows, axis=0), jnp.concatenate(grads, axis=0)
    over_rows = lambda g: lax.dot_general(all_rows, g, (((0,), (0,)), ((), ())), preferred_element_type=F32)
    theirs = swap(over_rows(all_grads[:, width:]), "C")
    head_grad = over_rows(all_grads[:, :width]) + theirs
    return (head_grad, input_grad)


def solution(mesh):
    placed = (
        P("dp", None),
        P("dp", None),
        P("dp"),
        P(None, ("dp", "tensor")),
        P(None, ("dp", "tensor")),
    )
    return jax.shard_map(
        body,
        mesh=mesh,
        in_specs=placed,
        out_specs=(P(None, ("dp", "tensor")), P("dp", "tensor")),
        check_vma=False,
    )
```

```python
import functools

import jax
import jax.numpy as jnp
from jax import lax
from jax.experimental import pallas as pl
from jax.experimental.pallas import tpu as pltpu
from jax.sharding import PartitionSpec as P

VOCAB = 64128
F32, BF16 = jnp.float32, jnp.bfloat16
AXES = ("dp", "tensor")

PARTS = (
    (0, 8, ("Zb", "Za"), ("X1", "Ya", "Yb", "Za", "Zb")),
    (48, 24, ("X0",), ("Yb", "Ya", "Xa", "Xb")),
    (96, 32, (), ("X1", "Ya", "Yb")),
    (32, 8, ("Zb",), ("Ya", "X1", "Yb", "Zb")),
)
WHOLE = (3,)
STAT_ORDER = ("Ya", "Za", "X0", "X1", "Zb", "Yb")
NARROW_STEPS = 3
GROUP = 8


def bits_of(dev):
    dp, tensor = dev // 8, dev % 8
    xh, y, core = dp // 8, (dp // 2) % 4, dp % 2
    xl, z = tensor // 4, tensor % 4
    gx, gy, gz = xh * 2 + (xh ^ xl), y ^ (y // 2), z ^ (z // 2)
    pick = lambda g, second: (g // 2) * second + (g % 2) * (1 - second)
    return {
        "X1": xh, "X0": xh ^ xl,
        "Xa": pick(gx, 1 - core), "Xb": pick(gx, core),
        "Ya": pick(gy, core), "Yb": pick(gy, 1 - core),
        "Za": pick(gz, core), "Zb": pick(gz, 1 - core),
        "C": core,
    }


def z_of(bits):
    core = bits["C"]
    high = bits["Zb"] * (1 - core) + bits["Za"] * core
    low = bits["Za"] * (1 - core) + bits["Zb"] * core
    return high * 2 + (high ^ low)


@functools.cache
def pairs(dim):
    if dim == "C":
        return [(d, d ^ 8) for d in range(128)]
    basis = ("X1", "X0", "Ya", "Yb", "Za", "Zb", "C")
    key = lambda b: tuple(b[k] for k in basis)
    table = {key(bits_of(d)): d for d in range(128)}
    out = []
    for d in range(128):
        b = bits_of(d)
        real = dim
        if dim in ("Xa", "Xb"):
            real = "X1" if (dim == "Xa") == (b["C"] == 0) else "X0"
        out.append((d, table[key(dict(b, **{real: 1 - b[real]}))]))
    return out


def swap(x, dim):
    return lax.ppermute(x, AXES, pairs(dim))


def flip(x, axis, pre):
    shape = x.shape
    n = shape[axis]
    y = x.reshape(shape[:axis] + (pre, 2, n // (2 * pre)) + shape[axis + 1 :])
    y = jnp.concatenate([lax.slice_in_dim(y, 1, 2, axis=axis + 1), lax.slice_in_dim(y, 0, 1, axis=axis + 1)], axis + 1)
    return y.reshape(shape)


def grad_kernel(counts, *refs):
    n = len(counts)
    place, turn, first = refs[:3]
    stats, ids = refs[3:5]
    z_refs = [refs[5 + 4 * i : 9 + 4 * i] for i in range(n)]
    own, other = refs[5 + 4 * n : 7 + 4 * n]
    g_own, g_other, u_keep, u_send, v_keep, v_send = refs[7 + 4 * n : 13 + 4 * n]
    plain, canon = refs[13 + 4 * n :]
    width = own.shape[1]

    at = 0
    for i, count in enumerate(counts):
        for lo in range(0, count, 64):
            rows = slice(at + lo, at + lo + 64)
            s = stats[rows, :]
            peak_t, peak_s, sum_t, sum_s = (s[:, j : j + 1] for j in range(4))
            digits = ids[rows, :].astype(F32)
            target = (digits[:, 0:1] * 256.0 + digits[:, 1:2]).astype(jnp.int32)
            for half in (0, 1):
                z_t = z_refs[i][half][lo : lo + 64, :]
                z_s = z_refs[i][2 + half][lo : lo + 64, :]
                column = first[half] + lax.broadcasted_iota(jnp.int32, (64, width), 1)
                onehot = jnp.where(target == column, F32(1), F32(0))
                p_t = jnp.exp(z_t - peak_t) * (1.0 / sum_t)
                p_s = jnp.exp(z_s - peak_s) * (1.0 / sum_s)
                g = (2.0 * p_s - p_t - onehot).astype(BF16)
                (g_own, g_other)[half][rows, :] = g
                plain[rows, half * width : (half + 1) * width] = g.astype(F32)
        at += count

    def put(i, _):
        canon[pl.ds(pl.multiple_of(place[i] * GROUP, GROUP), GROUP), :] = plain[
            pl.ds(pl.multiple_of(i * GROUP, GROUP), GROUP), :
        ]
        return 0

    lax.fori_loop(0, at // GROUP, put, 0, unroll=4)

    wide = u_keep.shape[-1]
    half_rows = at // 2
    for h in (0, 1):
        block = canon[h * half_rows : (h + 1) * half_rows, :].astype(BF16)
        for x in (0, 1):
            for zb in (0, 1):
                for za in (0, 1):
                    where = pl.multiple_of(turn[(x ^ h) * 4 + zb * 2 + za] * wide, wide)
                    dims = (((1,), (1,)), ((), ()))
                    r = lax.dot_general(block[:, :width], own[pl.ds(where, wide), :], dims, preferred_element_type=F32)
                    r += lax.dot_general(block[:, width:], other[pl.ds(where, wide), :], dims, preferred_element_type=F32)
                    r = r.reshape(2, 2, half_rows // 4, wide)
                    cut = u_keep.shape[-2]
                    if zb == 0:
                        u_keep[x, za, h] = r[:, :, :cut]
                    else:
                        u_send[x, za, h] = r[:, :, :cut].astype(BF16)
                    v_keep[x, zb, za, h] = r[0, :, cut:]
                    v_send[x, zb, za, h] = r[1, :, cut:].astype(BF16)


def body(teacher_hidden, student_hidden, target_ids, teacher_head, student_head):
    dev = lax.axis_index("dp") * 8 + lax.axis_index("tensor")
    bit = bits_of(dev)
    width = teacher_head.shape[1]
    per = teacher_hidden.shape[0]
    dt, ds = teacher_hidden.shape[1], student_hidden.shape[1]

    ids = jnp.stack([target_ids // 256, target_ids % 256], axis=1).astype(BF16)
    own = jnp.concatenate([teacher_hidden, student_hidden, jnp.pad(ids, ((0, 0), (0, 126)))], axis=1)

    state, axes_of = [], [list(order[::-1]) for *_, order in PARTS]
    for first, n, slices, _ in PARTS:
        index = 0
        for d in slices:
            index = index * 2 + bit[d]
        state.append([lax.dynamic_slice_in_dim(own, first + index * n, n, 0) if slices else own[first : first + n]])
    for step in range(5):
        if step == 1:
            state, teacher_head, student_head = lax.optimization_barrier((state, teacher_head, student_head))
            student_other, teacher_other = swap(student_head, "C"), swap(teacher_head, "C")
        if step == 3:
            state, student_other, teacher_other = lax.optimization_barrier((state, student_other, teacher_other))
        for i, (_, _, _, order) in enumerate(PARTS):
            if step < len(order):
                x = state[i][0]
                state[i] = [x, swap(x, order[step])]
                if step < len(order) - 1 or i in WHOLE:
                    state[i] = [jnp.concatenate(state[i], axis=0)]

    place = []
    for i, (first, n, slices, order) in enumerate(PARTS):
        total = n << len(order)
        for row in range(0, total, GROUP):
            rel, rest = {}, row // n
            for d in order:
                rel[d] = rest & 1
                rest >>= 1
            if "Xa" in rel:
                a, b = rel["Xa"], rel["Xb"]
                rel["X1"] = jnp.where(bit["C"] == 0, a, b)
                rel["X0"] = jnp.where(bit["C"] == 0, b, a)
            index = 0
            for d in slices:
                index = index * 2 + (rel[d] ^ bit[d])
            spot = (rel["X1"] * 4 + rel["Yb"] * 2 + rel["Ya"]) * per + first + index * n + row % n
            place.append(jnp.int32(spot // GROUP))
    place = jnp.stack(place)
    turn = []
    for x0 in (0, 1):
        for zb in (0, 1):
            for za in (0, 1):
                xl = bit["X0"] ^ x0 ^ bit["X1"]
                z = z_of({"C": bit["C"], "Zb": bit["Zb"] ^ zb, "Za": bit["Za"] ^ za})
                turn.append(jnp.int32(xl * 4 + z))
    turn = jnp.stack(turn)
    firsts = jnp.stack([dev * width, (dev ^ 8) * width]).astype(jnp.int32)
    real = [(firsts[i] + lax.iota(jnp.int32, width) < VOCAB)[None, :] for i in (0, 1)]

    logits, stats, counts, rows, digits = [], [], [], [], []
    for chunk in state:
        tops, sums = [], []
        for x in chunk:
            xt, xs = x[:, :dt], x[:, dt : dt + ds]
            z_t = [jnp.dot(xt, w, preferred_element_type=F32) for w in (teacher_head, teacher_other)]
            z_s = [jnp.dot(xs, w, preferred_element_type=F32) for w in (student_head, student_other)]
            z_t, z_s = ([jnp.where(r, z, F32(-1e30)) for r, z in zip(real, zs)] for zs in (z_t, z_s))
            for zs in (z_t, z_s):
                top = jnp.maximum(jnp.max(zs[0], axis=1), jnp.max(zs[1], axis=1))
                tops.append(top)
                sums.append(sum(jnp.sum(jnp.exp(z - top[:, None]), axis=1) for z in zs))
            logits += z_t + z_s
            counts.append(x.shape[0])
            rows.append(xs)
            digits.append(x[:, dt + ds :])
        stats.append([jnp.concatenate(v[j::2]) for v in (tops, sums) for j in (0, 1)])

    edge = [0]
    for s in stats:
        edge.append(edge[-1] + s[0].shape[0])
    both = jnp.stack([jnp.concatenate([s[j] for s in stats]) for j in range(4)])
    for d in STAT_ORDER:
        got = swap(both, d)
        pieces = []
        for i, axes in enumerate(axes_of):
            piece = got[:, edge[i] : edge[i + 1]]
            if d in axes:
                piece = flip(piece, 1, 1 << axes.index(d))
            elif d in ("X0", "X1") and "Xa" in axes:
                a, b = (flip(piece, 1, 1 << axes.index(k)) for k in ("Xa", "Xb"))
                piece = jnp.where(bit["C"] == (0 if d == "X1" else 1), a, b)
            pieces.append(piece)
        got = jnp.concatenate(pieces, axis=1)
        top = jnp.maximum(both[:2], got[:2])
        both = jnp.concatenate(
            [top, both[2:] * jnp.exp(both[:2] - top) + got[2:] * jnp.exp(got[:2] - top)], axis=0
        )

    total, wide, cut = edge[-1], ds // 8, per // 2
    vmem = pl.BlockSpec(memory_space=pltpu.VMEM)
    smem = pl.BlockSpec(memory_space=pltpu.SMEM)
    shape = jax.ShapeDtypeStruct
    u, v = (2, 2, 2, 2, 2, cut, wide), (2, 2, 2, 2, 2, per - cut, wide)
    g_own, g_other, u_keep, u_send, v_keep, v_send = pl.pallas_call(
        functools.partial(grad_kernel, tuple(counts)),
        out_shape=[
            shape((total, width), BF16), shape((total, width), BF16),
            shape(u, F32), shape(u, BF16), shape(v, F32), shape(v, BF16),
        ],
        in_specs=[smem] * 3 + [vmem] * (4 + len(logits)),
        out_specs=[vmem] * 6,
        scratch_shapes=[pltpu.VMEM((total, 2 * width), F32), pltpu.VMEM((total, 2 * width), F32)],
        compiler_params=pltpu.CompilerParams(vmem_limit_bytes=56 * 2**20),
        name="grad",
    )(place, turn, firsts, both.T, jnp.concatenate(digits, axis=0), *logits, student_head, student_other)

    all_rows = jnp.concatenate(rows, axis=0)
    over_rows = lambda g: lax.dot_general(all_rows, g, (((0,), (0,)), ((), ())), preferred_element_type=F32)

    streams = [
        [u_keep, u_send, ["X0", "Za", "X1", "Yb", "Ya"], ("Zb", "Yb", "Za", "Ya", "X1", "X0")],
        [v_keep, v_send, ["X0", "Zb", "Za", "X1", "Ya"], ("Yb", "Zb", "Ya", "Za", "X1", "X0")],
    ]
    head_grad = None
    for step in range(6):
        if step == 1:
            theirs = swap(over_rows(g_other), "C")
        if step == 3:
            head_grad = over_rows(g_own) + theirs
            streams[0][1], streams[1][1], head_grad = lax.optimization_barrier((streams[0][1], streams[1][1], head_grad))
        back = [swap(s[1], s[3][step]).astype(F32) for s in streams]
        for s, got in zip(streams, back):
            new = s[0] + got
            if step == 5:
                s[0] = new
                continue
            axis = s[2].index(s[3][step + 1])
            s[0], send = (lax.index_in_dim(new, j, axis, keepdims=False) for j in (0, 1))
            s[1] = send.astype(BF16) if step + 1 < NARROW_STEPS else send
            s[2].pop(axis)
    input_grad = jnp.concatenate([s[0] for s in streams], axis=0)
    return (head_grad, input_grad)


def solution(mesh):
    placed = (
        P("dp", None),
        P("dp", None),
        P("dp"),
        P(None, ("dp", "tensor")),
        P(None, ("dp", "tensor")),
    )
    return jax.shard_map(
        body,
        mesh=mesh,
        in_specs=placed,
        out_specs=(P(None, ("dp", "tensor")), P("dp", "tensor")),
        check_vma=False,
    )
```

```python
import functools

import jax
import jax.numpy as jnp
from jax import lax
from jax.experimental import pallas as pl
from jax.experimental.pallas import tpu as pltpu
from jax.sharding import PartitionSpec as P

VOCAB = 64128
F32, BF16 = jnp.float32, jnp.bfloat16
AXES = ("dp", "tensor")

PARTS = (
    (0, 24, ("Zb",), ("X1", "Ya", "Yb", "Zb")),
    (48, 24, ("X0",), ("Ya", "Yb", "Xa", "Xb")),
    (96, 32, (), (None, "X1", "Ya", "Yb")),
)
STAT_ORDER = ("Ya", "Za", "X0", "X1", "Zb", "Yb")
NARROW_STEPS = 3
GROUP = 8
TALL = 32
SLAB = 1024


def bits_of(dev):
    dp, tensor = dev // 8, dev % 8
    xh, y, core = dp // 8, (dp // 2) % 4, dp % 2
    xl, z = tensor // 4, tensor % 4
    gx, gy, gz = xh * 2 + (xh ^ xl), y ^ (y // 2), z ^ (z // 2)
    pick = lambda g, second: (g // 2) * second + (g % 2) * (1 - second)
    return {
        "X1": xh, "X0": xh ^ xl,
        "Xa": pick(gx, 1 - core), "Xb": pick(gx, core),
        "Ya": pick(gy, core), "Yb": pick(gy, 1 - core),
        "Za": pick(gz, core), "Zb": pick(gz, 1 - core),
        "C": core,
    }


def z_of(bits):
    core = bits["C"]
    high = bits["Zb"] * (1 - core) + bits["Za"] * core
    low = bits["Za"] * (1 - core) + bits["Zb"] * core
    return high * 2 + (high ^ low)


@functools.cache
def pairs(dim):
    if dim == "C":
        return [(d, d ^ 8) for d in range(128)]
    basis = ("X1", "X0", "Ya", "Yb", "Za", "Zb", "C")
    key = lambda b: tuple(b[k] for k in basis)
    table = {key(bits_of(d)): d for d in range(128)}
    out = []
    for d in range(128):
        b = bits_of(d)
        real = dim
        if dim in ("Xa", "Xb"):
            real = "X1" if (dim == "Xa") == (b["C"] == 0) else "X0"
        out.append((d, table[key(dict(b, **{real: 1 - b[real]}))]))
    return out


def swap(x, dim):
    return lax.ppermute(x, AXES, pairs(dim))


def logits_kernel(counts, last, place, first, *refs):
    n = len(counts)
    x_refs = refs[:n]
    heads = refs[n : n + 4]
    earlier = refs[n + 4 : n + 6]
    e_t, e_s, rows_out, stats, targets, canon, lines, x, w_t, w_s, z_t, z_s, sems = refs[n + 4 + 2 * last :]
    dt, ds, width = w_t.shape[0], w_s.shape[0], heads[0].shape[1]
    total = sum(counts)
    copies = []

    def copy(src, dst):
        copies.append(pltpu.make_async_copy(src, dst, sems.at[len(copies)]))
        copies[-1].start()
        return copies[-1]

    def rows_in(cols):
        out, at = [], 0
        for ref, count in zip(x_refs, counts):
            out.append(copy(ref.at[:, cols], x.at[pl.ds(at, count), cols]))
            at += count
        return out

    def slabs_in(own, other, w, depth):
        return [
            [
                copy(head.at[pl.ds(lo, SLAB), :], w.at[pl.ds(lo, SLAB), pl.ds(half * width, width)])
                for half, head in enumerate((own, other))
            ]
            for lo in range(0, depth, SLAB)
        ]

    x_s = rows_in(pl.ds(dt, x.shape[1] - dt))
    in_s = slabs_in(heads[2], heads[3], w_s, ds)
    x_t = rows_in(pl.ds(0, dt))
    in_t = slabs_in(heads[0], heads[1], w_t, dt)
    outs = []
    canon[...] = jnp.zeros_like(canon)
    lane = lax.broadcasted_iota(jnp.int32, (TALL, 128), 1)
    lane_width = lax.broadcasted_iota(jnp.int32, (1, width), 1)
    real = jnp.concatenate([first[half] + lane_width < VOCAB for half in (0, 1)], axis=1)

    def products(arrived, lo, w, z):
        for k, slab in enumerate(arrived):
            for c in slab:
                c.wait()
            for left in range(0, 2 * width, 256):
                r = jnp.dot(
                    x[:, lo + k * SLAB : lo + (k + 1) * SLAB],
                    w[k * SLAB : (k + 1) * SLAB, left : left + 256],
                    preferred_element_type=F32,
                )
                z[:, left : left + 256] = r if k == 0 else z[:, left : left + 256] + r

    def exponentials(z, rows):
        value = jnp.where(real, z[rows, :], F32(-1e30))
        top = jnp.max(value, axis=1, keepdims=True)
        e = jnp.exp(value - top)
        z[rows, :] = e
        return top, jnp.sum(e, axis=1, keepdims=True)

    for c in x_s:
        c.wait()
    outs.append(copy(x.at[:, pl.ds(dt, ds)], rows_out))
    products(in_s, dt, w_s, z_s)
    for lo in range(0, total, TALL):
        rows = slice(lo, lo + TALL)
        digits = x[rows, dt + ds :].astype(F32)
        m_s, n_s = exponentials(z_s, rows)
        line = jnp.where(lane == 1, m_s, 0.0)
        line = jnp.where(lane == 3, n_s, line)
        lines[rows, :] = jnp.where(lane == 4, digits[:, 0:1] * 256.0 + digits[:, 1:2], line)
    outs.append(copy(z_s, e_s))
    for c in x_t:
        c.wait()
    products(in_t, 0, w_t, z_t)
    for lo in range(0, total, TALL):
        rows = slice(lo, lo + TALL)
        m_t, n_t = exponentials(z_t, rows)
        line = jnp.where(lane == 0, m_t, lines[rows, :])
        line = jnp.where(lane == 2, n_t, line)
        for k in range(0, TALL, GROUP):
            spot = pl.multiple_of(place[(lo + k) // GROUP] * GROUP, GROUP)
            canon[pl.ds(spot, GROUP), :] = line[k : k + GROUP, :]
        if (lo + TALL) % 128 == 0:
            part = pl.ds(lo + TALL - 128, 128)
            outs.append(copy(z_t.at[part, :], e_t.at[part, :]))
    for i in range(8):
        across = canon[i * 128 : (i + 1) * 128, :].T
        for j in range(5):
            out, old = (stats.at[j], earlier[0].at[j] if last else None) if j < 4 else (targets, earlier[1] if last else None)
            value = across[j : j + 1, :]
            out[i : i + 1, :] = value + old[i : i + 1, :] if last else value
    for c in outs:
        c.wait()


def logits(chunks, place, firsts, heads, earlier=()):
    counts = tuple(x.shape[0] for x in chunks)
    total, rows = sum(counts), 2 * sum(counts)
    dt, (ds, width) = heads[0].shape[0], heads[2].shape
    shape = jax.ShapeDtypeStruct
    smem, vmem, far = (pl.BlockSpec(memory_space=m) for m in (pltpu.SMEM, pltpu.VMEM, pl.ANY))
    n_copies = 2 * len(chunks) + 2 * (dt + ds) // SLAB + 2 + total // 128
    return pl.pallas_call(
        functools.partial(logits_kernel, counts, bool(earlier)),
        out_shape=[
            shape((total, 2 * width), F32), shape((total, 2 * width), F32), shape((total, ds), BF16),
            shape((4, 8, 128), F32), shape((8, 128), F32),
        ],
        in_specs=[smem] * 2 + [far] * (len(chunks) + 4) + [vmem] * len(earlier),
        out_specs=[far] * 3 + [vmem] * 2,
        scratch_shapes=[
            pltpu.VMEM((rows, 128), F32),
            pltpu.VMEM((total, 128), F32),
            pltpu.VMEM((total, chunks[0].shape[1]), BF16),
            pltpu.VMEM((dt, 2 * width), BF16),
            pltpu.VMEM((ds, 2 * width), BF16),
            pltpu.VMEM((total, 2 * width), F32),
            pltpu.VMEM((total, 2 * width), F32),
            pltpu.SemaphoreType.DMA((n_copies,)),
        ],
        compiler_params=pltpu.CompilerParams(vmem_limit_bytes=56 * 2**20),
        cost_estimate=pl.CostEstimate(flops=10**11, bytes_accessed=0, transcendentals=0),
        name="logits",
    )(place, firsts, *chunks, *heads, *earlier)


def merge(mine, got):
    top = jnp.maximum(mine[:2], got[:2])
    sums = mine[2:] * jnp.exp(mine[:2] - top) + got[2:] * jnp.exp(got[:2] - top)
    return jnp.concatenate([top, sums], axis=0)


def grad_kernel(place, spots, turn, first, stats, local, targets, *refs):
    e_hbm, heads, outs = refs[:4], refs[4:6], refs[6:12]
    g_own, g_other, u_keep, u_send, v_keep, v_send = refs[12:18]
    canon, block, scales, e_all, w, sems = refs[18:]
    width = heads[0].shape[1]
    half_total = e_hbm[0].shape[0]
    total = 2 * half_total
    copies = []

    def copy(src, dst):
        copies.append(pltpu.make_async_copy(src, dst, sems.at[len(copies)]))
        copies[-1].start()
        return copies[-1]

    in_e = [copy(e_hbm[i], e_all.at[i]) for i in range(4)]
    in_w = [copy(head, w.at[:, pl.ds(i * width, width)]) for i, head in enumerate(heads)]
    row = lax.broadcasted_iota(jnp.int32, (128, 128), 0)
    for i in range(8):
        tile = jnp.where(row == 2, targets[i : i + 1, :], 0.0)
        for j in (0, 1):
            scale = jnp.exp(local[j, i : i + 1, :] - stats[j, i : i + 1, :]) / stats[2 + j, i : i + 1, :]
            tile = jnp.where(row == j, (1.0 + j) * scale, tile)
        scales[i * 128 : (i + 1) * 128, :] = tile.T

    for call in (0, 1):
        in_e[2 * call].wait()
        in_e[2 * call + 1].wait()
        e_t, e_s = e_all.at[2 * call], e_all.at[2 * call + 1]

        def rows16(i, _):
            here = pl.multiple_of(i * 16, 16)
            groups = [call * (half_total // GROUP) + 2 * i + k for k in (0, 1)]
            there = [pl.multiple_of(place[g] * GROUP, GROUP) for g in groups]
            s = jnp.concatenate(
                [scales[pl.ds(pl.multiple_of(spots[g] * GROUP, GROUP), GROUP), :] for g in groups], axis=0
            )
            target = s[:, 2:3].astype(jnp.int32)
            for half, out in ((0, g_own), (1, g_other)):
                cols = slice(half * width, (half + 1) * width)
                column = first[half] + lax.broadcasted_iota(jnp.int32, (16, width), 1)
                g = e_s[pl.ds(here, 16), cols] * s[:, 1:2] - e_t[pl.ds(here, 16), cols] * s[:, 0:1]
                g = jnp.where(target == column, g - 1.0, g)
                out[pl.ds(pl.multiple_of(call * half_total + here, 16), 16), :] = g.astype(BF16)
                for k in (0, 1):
                    canon[pl.ds(there[k], GROUP), cols] = g[k * GROUP : (k + 1) * GROUP, :]
            return 0

        lax.fori_loop(0, half_total // 16, rows16, 0, unroll=4)
    waits = [copy(g_own, outs[0]), copy(g_other, outs[1])]
    block[...] = canon[...].astype(BF16)
    for c in in_w:
        c.wait()

    wide, cut = u_keep.shape[-1], u_keep.shape[-2]
    for zb in (1, 0):
        for za in (1, 0):
            for x0 in (1, 0):
                where = pl.multiple_of(turn[x0 * 4 + zb * 2 + za] * wide, wide)
                r = lax.dot_general(
                    block[...], w[pl.ds(where, wide), :], (((1,), (1,)), ((), ())), preferred_element_type=F32
                ).reshape(2, 2, 2, total // 8, wide)
                for h in (0, 1):
                    x = x0 ^ h
                    if zb == 0:
                        u_keep[x, za, h] = r[h, :, :, :cut]
                        waits.append(copy(u_keep.at[x, za, h], outs[2].at[x, za, h]))
                    else:
                        u_send[x, za, h] = r[h, :, :, :cut].astype(BF16)
                        waits.append(copy(u_send.at[x, za, h], outs[3].at[x, za, h]))
                    v_keep[x, zb, za, h] = r[h, 0, :, cut:]
                    v_send[x, zb, za, h] = r[h, 1, :, cut:].astype(BF16)
                    waits.append(copy(v_keep.at[x, zb, za, h], outs[4].at[x, zb, za, h]))
                    waits.append(copy(v_send.at[x, zb, za, h], outs[5].at[x, zb, za, h]))
    for c in waits:
        c.wait()


def head_kernel(*refs):
    rows, (g, g_other), out = refs[:4], refs[4:6], refs[6]
    n = rows[0].shape[0]
    total = None
    for i, r in enumerate(rows):
        part = (g, g_other)[i // 2][(i % 2) * n : (i % 2 + 1) * n, :]
        product = lax.dot_general(r[...], part, (((0,), (0,)), ((), ())), preferred_element_type=F32)
        total = product if total is None else total + product
    out[...] = total


def head_gradient(rows, g, g_other):
    n, ds = rows[0].shape
    width = g.shape[1]
    tile = 256
    tall = pl.BlockSpec((n, tile), lambda i: (0, i))
    whole = pl.BlockSpec(g.shape, lambda i: (0, 0))
    return pl.pallas_call(
        head_kernel,
        grid=(ds // tile,),
        out_shape=jax.ShapeDtypeStruct((ds, width), F32),
        in_specs=[tall] * 4 + [whole] * 2,
        out_specs=pl.BlockSpec((tile, width), lambda i: (i, 0)),
        compiler_params=pltpu.CompilerParams(vmem_limit_bytes=32 * 2**20),
        cost_estimate=pl.CostEstimate(flops=10**11, bytes_accessed=0, transcendentals=0),
        name="head",
    )(*rows, g, g_other)


def body(teacher_hidden, student_hidden, target_ids, teacher_head, student_head):
    dev = lax.axis_index("dp") * 8 + lax.axis_index("tensor")
    bit = bits_of(dev)
    width = teacher_head.shape[1]
    per = teacher_hidden.shape[0]
    dt, ds = teacher_hidden.shape[1], student_hidden.shape[1]

    ids = jnp.stack([target_ids // 256, target_ids % 256], axis=1).astype(BF16)
    own = jnp.concatenate([teacher_hidden, student_hidden, jnp.pad(ids, ((0, 0), (0, 126)))], axis=1)

    state = []
    for first, n, slices, _ in PARTS:
        index = 0
        for d in slices:
            index = index * 2 + bit[d]
        state.append([lax.dynamic_slice_in_dim(own, first + index * n, n, 0) if slices else own[first : first + n]])
    student_other, teacher_other = swap(student_head, "C"), swap(teacher_head, "C")
    for step in range(4):
        if step == 2:
            state, student_other, teacher_other = lax.optimization_barrier((state, student_other, teacher_other))
        elif step:
            state = lax.optimization_barrier(state)
        for i, (_, _, _, order) in enumerate(PARTS):
            if order[step] is not None:
                x = state[i][0]
                state[i] = [x, swap(x, order[step])]
                if step < 3:
                    state[i] = [jnp.concatenate(state[i], axis=0)]

    place, spots = [[], []], [[], []]
    for i, (first, n, slices, order) in enumerate(PARTS):
        order = [d for d in order if d]
        total = n << len(order)
        for row in range(0, total, GROUP):
            rel, rest = {}, row // n
            for d in order:
                rel[d] = rest & 1
                rest >>= 1
            if "Xa" in rel:
                a, b = rel["Xa"], rel["Xb"]
                rel["X1"] = jnp.where(bit["C"] == 0, a, b)
                rel["X0"] = jnp.where(bit["C"] == 0, b, a)
            index = 0
            for d in slices:
                index = index * 2 + (rel[d] ^ bit[d])
            spot = (rel["X1"] * 4 + rel["Yb"] * 2 + rel["Ya"]) * per + first + index * n + row % n
            place[row >= total // 2].append(jnp.int32(spot // GROUP))
            block = sum((rel[d] ^ bit[d]) * k for d, k in (("X1", 4), ("Yb", 2), ("Ya", 1)))
            spots[row >= total // 2].append(jnp.int32((spot % per + block * per) // GROUP))
    place, spots = ([jnp.stack(p) for p in v] for v in (place, spots))
    turn = []
    for x0 in (0, 1):
        for zb in (0, 1):
            for za in (0, 1):
                xl = bit["X0"] ^ x0 ^ bit["X1"]
                z = z_of({"C": bit["C"], "Zb": bit["Zb"] ^ zb, "Za": bit["Za"] ^ za})
                turn.append(jnp.int32(xl * 4 + z))
    turn = jnp.stack(turn)
    firsts = jnp.stack([dev * width, (dev ^ 8) * width]).astype(jnp.int32)

    heads = (teacher_head, teacher_other, student_head, student_other)
    e_t0, e_s0, rows0, stats, targets = logits([x[0] for x in state], spots[0], firsts, heads)
    rows0_other = swap(rows0, "C")
    e_t1, e_s1, rows1, stats, targets = logits([x[1] for x in state], spots[1], firsts, heads, (stats, targets))
    local = stats
    for d in STAT_ORDER:
        stats = merge(stats, swap(stats, d))
    rows1_other = swap(rows1, "C")

    total, wide, cut = 2 * rows0.shape[0], ds // 8, per // 2
    vmem = pl.BlockSpec(memory_space=pltpu.VMEM)
    smem = pl.BlockSpec(memory_space=pltpu.SMEM)
    shape = jax.ShapeDtypeStruct
    u, v = (2, 2, 2, 2, 2, cut, wide), (2, 2, 2, 2, 2, per - cut, wide)
    outs = [((total, width), BF16)] * 2 + [(u, F32), (u, BF16), (v, F32), (v, BF16)]
    far = pl.BlockSpec(memory_space=pl.ANY)
    g_own, g_other, u_keep, u_send, v_keep, v_send = pl.pallas_call(
        grad_kernel,
        out_shape=[shape(*o) for o in outs],
        in_specs=[smem] * 4 + [vmem] * 3 + [far] * 6,
        out_specs=[far] * 6,
        scratch_shapes=[pltpu.VMEM(*o) for o in outs]
        + [
            pltpu.VMEM((total, 2 * width), F32),
            pltpu.VMEM((total, 2 * width), BF16),
            pltpu.VMEM((total, 128), F32),
            pltpu.VMEM((4, total // 2, 2 * width), F32),
            pltpu.VMEM((ds, 2 * width), BF16),
            pltpu.SemaphoreType.DMA((8 + 6 * 8,)),
        ],
        compiler_params=pltpu.CompilerParams(vmem_limit_bytes=56 * 2**20),
        name="grad",
    )(
        jnp.concatenate(place), jnp.concatenate(spots), turn, firsts, stats, local, targets,
        e_t0, e_s0, e_t1, e_s1, student_head, student_other,
    )
    head_grad = head_gradient((rows0, rows1, rows0_other, rows1_other), g_own, swap(g_other, "C"))

    streams = [
        [u_keep, u_send, ["X0", "Za", "X1", "Yb", "Ya"], ("Zb", "Yb", "Za", "Ya", "X1", "X0")],
        [v_keep, v_send, ["X0", "Zb", "Za", "X1", "Ya"], ("Yb", "Zb", "Ya", "Za", "X1", "X0")],
    ]
    for step in range(6):
        back = [swap(s[1], s[3][step]) for s in streams]
        if step == 0:
            back[0], back[1], head_grad = lax.optimization_barrier((back[0], back[1], head_grad))
        back = [got.astype(F32) for got in back]
        for s, got in zip(streams, back):
            new = s[0] + got
            if step == 5:
                s[0] = new
                continue
            axis = s[2].index(s[3][step + 1])
            s[0], send = (lax.index_in_dim(new, j, axis, keepdims=False) for j in (0, 1))
            s[1] = send.astype(BF16) if step + 1 < NARROW_STEPS else send
            s[2].pop(axis)
    input_grad = jnp.concatenate([s[0] for s in streams], axis=0)
    return (head_grad, input_grad)


def solution(mesh):
    placed = (
        P("dp", None),
        P("dp", None),
        P("dp"),
        P(None, ("dp", "tensor")),
        P(None, ("dp", "tensor")),
    )
    return jax.shard_map(
        body,
        mesh=mesh,
        in_specs=placed,
        out_specs=(P(None, ("dp", "tensor")), P("dp", "tensor")),
        check_vma=False,
    )
```

```python
import functools

import jax
import jax.numpy as jnp
import numpy as np
from jax import lax
from jax.experimental import pallas as pl
from jax.experimental.pallas import tpu as pltpu
from jax.sharding import PartitionSpec as P

VOCAB = 64128
F32, BF16 = jnp.float32, jnp.bfloat16
AXES = ("dp", "tensor")

PARTS = (
    (0, 24, ("Zb",), ("X1", "Ya", "Zb", "Yb")),
    (48, 24, ("X0",), ("Ya", "Yb", "Xa", "Xb")),
    (96, 16, ("Za",), ("Ya", "X1", "Yb", "Za")),
)
CALLS = (((0, 0), (1, 0), (2, 0)), ((2, 1),), ((0, 1), (1, 1)))
STAT_ORDER = ("Ya", "Za", "X0", "X1", "Zb", "Yb")
NARROW_STEPS = 4
GROUP = 8
TALL = 32
SLAB = 1024


def bits_of(dev):
    dp, tensor = dev // 8, dev % 8
    xh, y, core = dp // 8, (dp // 2) % 4, dp % 2
    xl, z = tensor // 4, tensor % 4
    gx, gy, gz = xh * 2 + (xh ^ xl), y ^ (y // 2), z ^ (z // 2)
    pick = lambda g, second: (g // 2) * second + (g % 2) * (1 - second)
    return {
        "X1": xh, "X0": xh ^ xl,
        "Xa": pick(gx, 1 - core), "Xb": pick(gx, core),
        "Ya": pick(gy, core), "Yb": pick(gy, 1 - core),
        "Za": pick(gz, core), "Zb": pick(gz, 1 - core),
        "C": core,
    }


def z_of(bits):
    core = bits["C"]
    high = bits["Zb"] * (1 - core) + bits["Za"] * core
    low = bits["Za"] * (1 - core) + bits["Zb"] * core
    return high * 2 + (high ^ low)


@functools.cache
def pairs(dim):
    if dim == "C":
        return [(d, d ^ 8) for d in range(128)]
    basis = ("X1", "X0", "Ya", "Yb", "Za", "Zb", "C")
    key = lambda b: tuple(b[k] for k in basis)
    table = {key(bits_of(d)): d for d in range(128)}
    out = []
    for d in range(128):
        b = bits_of(d)
        real = dim
        if dim in ("Xa", "Xb"):
            real = "X1" if (dim == "Xa") == (b["C"] == 0) else "X0"
        out.append((d, table[key(dict(b, **{real: 1 - b[real]}))]))
    return out


def swap(x, dim):
    return lax.ppermute(x, AXES, pairs(dim))


def logits_kernel(counts, last, place, first, *refs):
    n = len(counts)
    x_refs = refs[:n]
    heads = refs[n : n + 4]
    earlier = refs[n + 4 : n + 6]
    e_t, e_s, rows_out, stats, targets, canon, lines, x, w_t, w_s, z_t, z_s, sems = refs[n + 4 + 2 * last :]
    dt, ds, width = w_t.shape[0], w_s.shape[0], heads[0].shape[1]
    total = sum(counts)
    copies = []

    def copy(src, dst):
        copies.append(pltpu.make_async_copy(src, dst, sems.at[len(copies)]))
        copies[-1].start()
        return copies[-1]

    def rows_in(cols):
        out, at = [], 0
        for ref, count in zip(x_refs, counts):
            out.append(copy(ref.at[:, cols], x.at[pl.ds(at, count), cols]))
            at += count
        return out

    def slabs_in(own, other, w, depth):
        return [
            [
                copy(head.at[pl.ds(lo, SLAB), :], w.at[pl.ds(lo, SLAB), pl.ds(half * width, width)])
                for half, head in enumerate((own, other))
            ]
            for lo in range(0, depth, SLAB)
        ]

    x_s = rows_in(pl.ds(dt, x.shape[1] - dt))
    in_s = slabs_in(heads[2], heads[3], w_s, ds)
    x_t = rows_in(pl.ds(0, dt))
    in_t = slabs_in(heads[0], heads[1], w_t, dt)
    outs = []
    canon[...] = jnp.zeros_like(canon)
    lane = lax.broadcasted_iota(jnp.int32, (TALL, 128), 1)
    lane_width = lax.broadcasted_iota(jnp.int32, (1, width), 1)
    real = jnp.concatenate([first[half] + lane_width < VOCAB for half in (0, 1)], axis=1)

    def products(arrived, lo, w, z):
        for k, slab in enumerate(arrived):
            for c in slab:
                c.wait()
            for left in range(0, 2 * width, 256):
                r = jnp.dot(
                    x[:, lo + k * SLAB : lo + (k + 1) * SLAB],
                    w[k * SLAB : (k + 1) * SLAB, left : left + 256],
                    preferred_element_type=F32,
                )
                z[:, left : left + 256] = r if k == 0 else z[:, left : left + 256] + r

    def exponentials(z, rows):
        value = jnp.where(real, z[rows, :], F32(-1e30))
        top = jnp.max(value, axis=1, keepdims=True)
        e = jnp.exp(value - top)
        z[rows, :] = e
        return top, jnp.sum(e, axis=1, keepdims=True)

    for c in x_s:
        c.wait()
    outs.append(copy(x.at[:, pl.ds(dt, ds)], rows_out))
    products(in_s, dt, w_s, z_s)
    for lo in range(0, total, TALL):
        rows = slice(lo, lo + TALL)
        digits = x[rows, dt + ds :].astype(F32)
        m_s, n_s = exponentials(z_s, rows)
        line = jnp.where(lane == 1, m_s, 0.0)
        line = jnp.where(lane == 3, n_s, line)
        lines[rows, :] = jnp.where(lane == 4, digits[:, 0:1] * 256.0 + digits[:, 1:2], line)
    outs.append(copy(z_s, e_s))
    for c in x_t:
        c.wait()
    products(in_t, 0, w_t, z_t)
    for lo in range(0, total, TALL):
        rows = slice(lo, lo + TALL)
        m_t, n_t = exponentials(z_t, rows)
        line = jnp.where(lane == 0, m_t, lines[rows, :])
        line = jnp.where(lane == 2, n_t, line)
        for k in range(0, TALL, GROUP):
            spot = pl.multiple_of(place[(lo + k) // GROUP] * GROUP, GROUP)
            canon[pl.ds(spot, GROUP), :] = line[k : k + GROUP, :]
        if (lo + TALL) % 128 == 0:
            part = pl.ds(lo + TALL - 128, 128)
            outs.append(copy(z_t.at[part, :], e_t.at[part, :]))
    for i in range(8):
        across = canon[i * 128 : (i + 1) * 128, :].T
        for j in range(5):
            out, old = (stats.at[j], earlier[0].at[j] if last else None) if j < 4 else (targets, earlier[1] if last else None)
            value = across[j : j + 1, :]
            out[i : i + 1, :] = value + old[i : i + 1, :] if last else value
    for c in outs:
        c.wait()


def logits(chunks, place, firsts, heads, rows, earlier):
    counts = tuple(x.shape[0] for x in chunks)
    total = sum(counts)
    dt, (ds, width) = heads[0].shape[0], heads[2].shape
    shape = jax.ShapeDtypeStruct
    smem, vmem, far = (pl.BlockSpec(memory_space=m) for m in (pltpu.SMEM, pltpu.VMEM, pl.ANY))
    n_copies = 2 * len(chunks) + 2 * (dt + ds) // SLAB + 2 + total // 128
    return pl.pallas_call(
        functools.partial(logits_kernel, counts, bool(earlier)),
        out_shape=[
            shape((total, 2 * width), F32), shape((total, 2 * width), F32), shape((total, ds), BF16),
            shape((4, 8, 128), F32), shape((8, 128), F32),
        ],
        in_specs=[smem] * 2 + [far] * (len(chunks) + 4) + [vmem] * len(earlier),
        out_specs=[far] * 3 + [vmem] * 2,
        scratch_shapes=[
            pltpu.VMEM((rows, 128), F32),
            pltpu.VMEM((total, 128), F32),
            pltpu.VMEM((total, chunks[0].shape[1]), BF16),
            pltpu.VMEM((dt, 2 * width), BF16),
            pltpu.VMEM((ds, 2 * width), BF16),
            pltpu.VMEM((total, 2 * width), F32),
            pltpu.VMEM((total, 2 * width), F32),
            pltpu.SemaphoreType.DMA((n_copies,)),
        ],
        compiler_params=pltpu.CompilerParams(vmem_limit_bytes=56 * 2**20),
        cost_estimate=pl.CostEstimate(flops=10**11, bytes_accessed=0, transcendentals=0),
        name="logits",
    )(place, firsts, *chunks, *heads, *earlier)


def merge(mine, got):
    top = jnp.maximum(mine[:2], got[:2])
    sums = mine[2:] * jnp.exp(mine[:2] - top) + got[2:] * jnp.exp(got[:2] - top)
    return jnp.concatenate([top, sums], axis=0)


def grad_kernel(place, spots, turn, first, stats, local, targets, *refs):
    n = 2 * len(CALLS)
    e_hbm, heads, outs = refs[:n], refs[n : n + 2], refs[n + 2 : n + 8]
    g_own, g_other, u_keep, u_send, v_keep, v_send = refs[n + 8 : n + 14]
    canon, block, scales, e_all, w, sems = refs[n + 14 :]
    width = heads[0].shape[1]
    total = canon.shape[0]
    copies = []

    def copy(src, dst):
        copies.append(pltpu.make_async_copy(src, dst, sems.at[len(copies)]))
        copies[-1].start()
        return copies[-1]

    in_e, edge = [], [0]
    for i, e in enumerate(e_hbm):
        in_e.append(copy(e, e_all.at[i % 2, pl.ds(edge[-1], e.shape[0]), :]))
        if i % 2:
            edge.append(edge[-1] + e.shape[0])
    in_w = [copy(head, w.at[:, pl.ds(i * width, width)]) for i, head in enumerate(heads)]
    row = lax.broadcasted_iota(jnp.int32, (128, 128), 0)
    for i in range(8):
        tile = jnp.where(row == 2, targets[i : i + 1, :], 0.0)
        for j in (0, 1):
            scale = jnp.exp(local[j, i : i + 1, :] - stats[j, i : i + 1, :]) / stats[2 + j, i : i + 1, :]
            tile = jnp.where(row == j, (1.0 + j) * scale, tile)
        scales[i * 128 : (i + 1) * 128, :] = tile.T

    for call in range(len(CALLS)):
        in_e[2 * call].wait()
        in_e[2 * call + 1].wait()

        def rows16(i, _):
            here = pl.multiple_of(i * 16, 16)
            groups = [2 * i + k for k in (0, 1)]
            there = [pl.multiple_of(place[g] * GROUP, GROUP) for g in groups]
            s = jnp.concatenate(
                [scales[pl.ds(pl.multiple_of(spots[g] * GROUP, GROUP), GROUP), :] for g in groups], axis=0
            )
            target = s[:, 2:3].astype(jnp.int32)
            for half, out in ((0, g_own), (1, g_other)):
                cols = slice(half * width, (half + 1) * width)
                column = first[half] + lax.broadcasted_iota(jnp.int32, (16, width), 1)
                g = e_all[1, pl.ds(here, 16), cols] * s[:, 1:2] - e_all[0, pl.ds(here, 16), cols] * s[:, 0:1]
                g = jnp.where(target == column, g - 1.0, g)
                out[pl.ds(here, 16), :] = g.astype(BF16)
                for k in (0, 1):
                    canon[pl.ds(there[k], GROUP), cols] = g[k * GROUP : (k + 1) * GROUP, :]
            return 0

        lax.fori_loop(edge[call] // 16, edge[call + 1] // 16, rows16, 0, unroll=4)
    waits = [copy(g_own, outs[0]), copy(g_other, outs[1])]
    block[...] = canon[...].astype(BF16)
    for c in in_w:
        c.wait()

    wide, cut = u_keep.shape[-1], u_keep.shape[-2]
    for zb in (1, 0):
        for za in (1, 0):
            for x0 in (1, 0):
                where = pl.multiple_of(turn[x0 * 4 + zb * 2 + za] * wide, wide)
                r = lax.dot_general(
                    block[...], w[pl.ds(where, wide), :], (((1,), (1,)), ((), ())), preferred_element_type=F32
                ).reshape(2, 2, 2, total // 8, wide)
                for h in (0, 1):
                    x = x0 ^ h
                    if zb == 0:
                        u_keep[x, za, h] = r[h, :, :, :cut]
                        waits.append(copy(u_keep.at[x, za, h], outs[2].at[x, za, h]))
                    else:
                        u_send[x, za, h] = r[h, :, :, :cut].astype(BF16)
                        waits.append(copy(u_send.at[x, za, h], outs[3].at[x, za, h]))
                    v_keep[x, zb, za, h] = r[h, 0, :, cut:]
                    v_send[x, zb, za, h] = r[h, 1, :, cut:].astype(BF16)
                    waits.append(copy(v_keep.at[x, zb, za, h], outs[4].at[x, zb, za, h]))
                    waits.append(copy(v_send.at[x, zb, za, h], outs[5].at[x, zb, za, h]))
    for c in waits:
        c.wait()


def head_kernel(*refs):
    *rows, g, g_other, out = refs
    total, at = None, 0
    for r in rows:
        n = r.shape[0]
        lo = at % g.shape[0]
        part = (g if at < g.shape[0] else g_other)[lo : lo + n, :]
        product = lax.dot_general(r[...], part, (((0,), (0,)), ((), ())), preferred_element_type=F32)
        total = product if total is None else total + product
        at += n
    out[...] = total


def head_gradient(rows, g, g_other):
    ds, (total, width) = rows[0].shape[1], g.shape
    tile = 256
    whole = pl.BlockSpec(g.shape, lambda i: (0, 0))
    return pl.pallas_call(
        head_kernel,
        grid=(ds // tile,),
        out_shape=jax.ShapeDtypeStruct((ds, width), F32),
        in_specs=[pl.BlockSpec((r.shape[0], tile), lambda i: (0, i)) for r in rows] + [whole] * 2,
        out_specs=pl.BlockSpec((tile, width), lambda i: (i, 0)),
        compiler_params=pltpu.CompilerParams(vmem_limit_bytes=32 * 2**20),
        cost_estimate=pl.CostEstimate(flops=10**11, bytes_accessed=0, transcendentals=0),
        name="head",
    )(*rows, g, g_other)


def body(teacher_hidden, student_hidden, target_ids, teacher_head, student_head):
    dev = lax.axis_index("dp") * 8 + lax.axis_index("tensor")
    bit = bits_of(dev)
    width = teacher_head.shape[1]
    per = teacher_hidden.shape[0]
    dt, ds = teacher_hidden.shape[1], student_hidden.shape[1]

    ids = jnp.stack([target_ids // 256, target_ids % 256], axis=1).astype(BF16)
    own = jnp.concatenate([teacher_hidden, student_hidden, jnp.pad(ids, ((0, 0), (0, 126)))], axis=1)

    state = []
    for first, n, slices, _ in PARTS:
        index = 0
        for d in slices:
            index = index * 2 + bit[d]
        state.append([lax.dynamic_slice_in_dim(own, first + index * n, n, 0) if slices else own[first : first + n]])
    student_other, teacher_other = swap(student_head, "C"), swap(teacher_head, "C")
    for step in range(4):
        if step == 2:
            state, student_other, teacher_other = lax.optimization_barrier((state, student_other, teacher_other))
        elif step:
            state = lax.optimization_barrier(state)
        for i, (_, _, _, order) in enumerate(PARTS):
            if order[step] is not None:
                x = state[i][0]
                state[i] = [x, swap(x, order[step])]
                if step < 3:
                    state[i] = [jnp.concatenate(state[i], axis=0)]

    place, spots = [], []
    for call in CALLS:
        for i, late in call:
            first, n, slices, order = PARTS[i]
            half = n << (len(order) - 1)
            row = np.arange(late * half, (late + 1) * half, GROUP)
            rel = {d: (row // n >> k & 1).astype(np.int32) for k, d in enumerate(order)}
            if "Xa" in rel:
                a, b = rel["Xa"], rel["Xb"]
                rel["X1"] = a * (1 - bit["C"]) + b * bit["C"]
                rel["X0"] = b * (1 - bit["C"]) + a * bit["C"]
            (d,) = slices
            inner = first + (rel[d] ^ bit[d]) * n + (row % n).astype(np.int32)
            near = (rel["X1"] * 4 + rel["Yb"] * 2 + rel["Ya"]) * per
            fixed = ((rel["X1"] ^ bit["X1"]) * 4 + (rel["Yb"] ^ bit["Yb"]) * 2 + (rel["Ya"] ^ bit["Ya"])) * per
            place.append((near + inner) // GROUP)
            spots.append((fixed + inner) // GROUP)
    place, spots = jnp.concatenate(place).astype(jnp.int32), jnp.concatenate(spots).astype(jnp.int32)
    turn = []
    for x0 in (0, 1):
        for zb in (0, 1):
            for za in (0, 1):
                xl = bit["X0"] ^ x0 ^ bit["X1"]
                z = z_of({"C": bit["C"], "Zb": bit["Zb"] ^ zb, "Za": bit["Za"] ^ za})
                turn.append(jnp.int32(xl * 4 + z))
    turn = jnp.stack(turn)
    firsts = jnp.stack([dev * width, (dev ^ 8) * width]).astype(jnp.int32)

    heads = (teacher_head, teacher_other, student_head, student_other)
    expos, rows, rows_other, side, at = [], [], [], (), 0
    for call in CALLS:
        chunks = [state[i][late] for i, late in call]
        n = sum(x.shape[0] for x in chunks)
        e_t, e_s, r, *side = logits(chunks, spots[at // GROUP : (at + n) // GROUP], firsts, heads, per * 8, side)
        expos += [e_t, e_s]
        rows.append(r)
        at += n
    rows_other = [swap(r, "C") for r in rows]
    stats, targets = side
    local = stats
    for d in STAT_ORDER:
        stats = merge(stats, swap(stats, d))

    total, wide, cut = at, ds // 8, per // 2
    vmem = pl.BlockSpec(memory_space=pltpu.VMEM)
    smem = pl.BlockSpec(memory_space=pltpu.SMEM)
    shape = jax.ShapeDtypeStruct
    u, v = (2, 2, 2, 2, 2, cut, wide), (2, 2, 2, 2, 2, per - cut, wide)
    outs = [((total, width), BF16)] * 2 + [(u, F32), (u, BF16), (v, F32), (v, BF16)]
    far = pl.BlockSpec(memory_space=pl.ANY)
    g_own, g_other, u_keep, u_send, v_keep, v_send = pl.pallas_call(
        grad_kernel,
        out_shape=[shape(*o) for o in outs],
        in_specs=[smem] * 4 + [vmem] * 3 + [far] * (len(expos) + 2),
        out_specs=[far] * 6,
        scratch_shapes=[pltpu.VMEM(*o) for o in outs]
        + [
            pltpu.VMEM((total, 2 * width), F32),
            pltpu.VMEM((total, 2 * width), BF16),
            pltpu.VMEM((total, 128), F32),
            pltpu.VMEM((2, total, 2 * width), F32),
            pltpu.VMEM((ds, 2 * width), BF16),
            pltpu.SemaphoreType.DMA((len(expos) + 4 + 6 * 8,)),
        ],
        compiler_params=pltpu.CompilerParams(vmem_limit_bytes=56 * 2**20),
        name="grad",
    )(
        place, spots, turn, firsts, stats, local, targets, *expos, student_head, student_other
    )
    head_grad = head_gradient(rows + rows_other, g_own, swap(g_other, "C"))

    streams = [
        [u_keep, u_send, ["X0", "Za", "X1", "Yb", "Ya"], ("Zb", "Yb", "Za", "Ya", "X1", "X0")],
        [v_keep, v_send, ["X0", "Zb", "Za", "X1", "Ya"], ("Yb", "Zb", "Ya", "Za", "X0", "X1")],
    ]
    for step in range(6):
        back = [swap(s[1], s[3][step]) for s in streams]
        if step == 0:
            back[0], back[1], head_grad = lax.optimization_barrier((back[0], back[1], head_grad))
        back = [got.astype(F32) for got in back]
        for s, got in zip(streams, back):
            new = s[0] + got
            if step == 5:
                s[0] = new
                continue
            axis = s[2].index(s[3][step + 1])
            s[0], send = (lax.index_in_dim(new, j, axis, keepdims=False) for j in (0, 1))
            s[1] = send.astype(BF16) if step + 1 < NARROW_STEPS else send
            s[2].pop(axis)
    input_grad = jnp.concatenate([s[0] for s in streams], axis=0)
    return (head_grad, input_grad)


def solution(mesh):
    placed = (
        P("dp", None),
        P("dp", None),
        P("dp"),
        P(None, ("dp", "tensor")),
        P(None, ("dp", "tensor")),
    )
    return jax.shard_map(
        body,
        mesh=mesh,
        in_specs=placed,
        out_specs=(P(None, ("dp", "tensor")), P("dp", "tensor")),
        check_vma=False,
    )
```

```python
import functools

import jax
import jax.numpy as jnp
import numpy as np
from jax import lax
from jax.experimental import pallas as pl
from jax.experimental.pallas import tpu as pltpu
from jax.sharding import PartitionSpec as P

VOCAB = 64128
F32, BF16 = jnp.float32, jnp.bfloat16
AXES = ("dp", "tensor")

PARTS = (
    (0, 24, ("Zb",), ("X1", "Ya", "Zb", "Yb")),
    (48, 24, ("X0",), ("Yb", "Ya", "Xa", "Xb")),
    (96, 16, ("Za",), ("Yb", "X1", "Ya", "Za")),
)
CALLS = (((0, 0), (1, 0), (2, 0)), ((2, 1),), ((0, 1), (1, 1)))
STAT_ORDER = ("Ya", "Za", "X0", "X1", "Zb", "Yb")
NARROW_STEPS = 4
GROUP = 8
TALL = 32
SLAB = 1024


def bits_of(dev):
    dp, tensor = dev // 8, dev % 8
    xh, y, core = dp // 8, (dp // 2) % 4, dp % 2
    xl, z = tensor // 4, tensor % 4
    gx, gy, gz = xh * 2 + (xh ^ xl), y ^ (y // 2), z ^ (z // 2)
    pick = lambda g, second: (g // 2) * second + (g % 2) * (1 - second)
    return {
        "X1": xh, "X0": xh ^ xl,
        "Xa": pick(gx, 1 - core), "Xb": pick(gx, core),
        "Ya": pick(gy, core), "Yb": pick(gy, 1 - core),
        "Za": pick(gz, core), "Zb": pick(gz, 1 - core),
        "C": core,
    }


def z_of(bits):
    core = bits["C"]
    high = bits["Zb"] * (1 - core) + bits["Za"] * core
    low = bits["Za"] * (1 - core) + bits["Zb"] * core
    return high * 2 + (high ^ low)


@functools.cache
def pairs(dim):
    if dim == "C":
        return [(d, d ^ 8) for d in range(128)]
    basis = ("X1", "X0", "Ya", "Yb", "Za", "Zb", "C")
    key = lambda b: tuple(b[k] for k in basis)
    table = {key(bits_of(d)): d for d in range(128)}
    out = []
    for d in range(128):
        b = bits_of(d)
        real = dim
        if dim in ("Xa", "Xb"):
            real = "X1" if (dim == "Xa") == (b["C"] == 0) else "X0"
        out.append((d, table[key(dict(b, **{real: 1 - b[real]}))]))
    return out


def swap(x, dim):
    return lax.ppermute(x, AXES, pairs(dim))


def logits_kernel(counts, last, place, first, *refs):
    n = len(counts)
    x_refs = refs[:n]
    heads = refs[n : n + 4]
    earlier = refs[n + 4 : n + 6]
    e_t, e_s, rows_out, stats, targets, canon, lines, x, w_t, w_s, z_t, z_s, sems = refs[n + 4 + 2 * last :]
    dt, ds, width = w_t.shape[0], w_s.shape[0], heads[0].shape[1]
    total = sum(counts)
    copies = []

    def copy(src, dst):
        copies.append(pltpu.make_async_copy(src, dst, sems.at[len(copies)]))
        copies[-1].start()
        return copies[-1]

    def rows_in(cols):
        out, at = [], 0
        for ref, count in zip(x_refs, counts):
            out.append(copy(ref.at[:, cols], x.at[pl.ds(at, count), cols]))
            at += count
        return out

    def slabs_in(own, other, w, depth):
        return [
            [
                copy(head.at[pl.ds(lo, SLAB), :], w.at[pl.ds(lo, SLAB), pl.ds(half * width, width)])
                for half, head in enumerate((own, other))
            ]
            for lo in range(0, depth, SLAB)
        ]

    x_s = rows_in(pl.ds(dt, x.shape[1] - dt))
    in_s = slabs_in(heads[2], heads[3], w_s, ds)
    x_t = rows_in(pl.ds(0, dt))
    in_t = slabs_in(heads[0], heads[1], w_t, dt)
    outs = []
    canon[...] = jnp.zeros_like(canon)
    lane = lax.broadcasted_iota(jnp.int32, (TALL, 128), 1)
    lane_width = lax.broadcasted_iota(jnp.int32, (1, width), 1)
    real = jnp.concatenate([first[half] + lane_width < VOCAB for half in (0, 1)], axis=1)

    def products(arrived, lo, w, z):
        for k, slab in enumerate(arrived):
            for c in slab:
                c.wait()
            for left in range(0, 2 * width, 256):
                r = jnp.dot(
                    x[:, lo + k * SLAB : lo + (k + 1) * SLAB],
                    w[k * SLAB : (k + 1) * SLAB, left : left + 256],
                    preferred_element_type=F32,
                )
                z[:, left : left + 256] = r if k == 0 else z[:, left : left + 256] + r

    def exponentials(z, rows):
        value = jnp.where(real, z[rows, :], F32(-1e30))
        top = jnp.max(value, axis=1, keepdims=True)
        e = jnp.exp(value - top)
        z[rows, :] = e
        return top, jnp.sum(e, axis=1, keepdims=True)

    for c in x_s:
        c.wait()
    outs.append(copy(x.at[:, pl.ds(dt, ds)], rows_out))
    products(in_s, dt, w_s, z_s)
    for lo in range(0, total, TALL):
        rows = slice(lo, lo + TALL)
        digits = x[rows, dt + ds :].astype(F32)
        m_s, n_s = exponentials(z_s, rows)
        line = jnp.where(lane == 1, m_s, 0.0)
        line = jnp.where(lane == 3, n_s, line)
        lines[rows, :] = jnp.where(lane == 4, digits[:, 0:1] * 256.0 + digits[:, 1:2], line)
    outs.append(copy(z_s, e_s))
    for c in x_t:
        c.wait()
    products(in_t, 0, w_t, z_t)
    for lo in range(0, total, TALL):
        rows = slice(lo, lo + TALL)
        m_t, n_t = exponentials(z_t, rows)
        line = jnp.where(lane == 0, m_t, lines[rows, :])
        line = jnp.where(lane == 2, n_t, line)
        for k in range(0, TALL, GROUP):
            spot = pl.multiple_of(place[(lo + k) // GROUP] * GROUP, GROUP)
            canon[pl.ds(spot, GROUP), :] = line[k : k + GROUP, :]
        if (lo + TALL) % 128 == 0:
            part = pl.ds(lo + TALL - 128, 128)
            outs.append(copy(z_t.at[part, :], e_t.at[part, :]))
    for i in range(8):
        across = canon[i * 128 : (i + 1) * 128, :].T
        for j in range(5):
            out, old = (stats.at[j], earlier[0].at[j] if last else None) if j < 4 else (targets, earlier[1] if last else None)
            value = across[j : j + 1, :]
            out[i : i + 1, :] = value + old[i : i + 1, :] if last else value
    for c in outs:
        c.wait()


def logits(chunks, place, firsts, heads, rows, earlier):
    counts = tuple(x.shape[0] for x in chunks)
    total = sum(counts)
    dt, (ds, width) = heads[0].shape[0], heads[2].shape
    shape = jax.ShapeDtypeStruct
    smem, vmem, far = (pl.BlockSpec(memory_space=m) for m in (pltpu.SMEM, pltpu.VMEM, pl.ANY))
    n_copies = 2 * len(chunks) + 2 * (dt + ds) // SLAB + 2 + total // 128
    return pl.pallas_call(
        functools.partial(logits_kernel, counts, bool(earlier)),
        out_shape=[
            shape((total, 2 * width), F32), shape((total, 2 * width), F32), shape((total, ds), BF16),
            shape((4, 8, 128), F32), shape((8, 128), F32),
        ],
        in_specs=[smem] * 2 + [far] * (len(chunks) + 4) + [vmem] * len(earlier),
        out_specs=[far] * 3 + [vmem] * 2,
        scratch_shapes=[
            pltpu.VMEM((rows, 128), F32),
            pltpu.VMEM((total, 128), F32),
            pltpu.VMEM((total, chunks[0].shape[1]), BF16),
            pltpu.VMEM((dt, 2 * width), BF16),
            pltpu.VMEM((ds, 2 * width), BF16),
            pltpu.VMEM((total, 2 * width), F32),
            pltpu.VMEM((total, 2 * width), F32),
            pltpu.SemaphoreType.DMA((n_copies,)),
        ],
        compiler_params=pltpu.CompilerParams(vmem_limit_bytes=56 * 2**20),
        cost_estimate=pl.CostEstimate(flops=10**11, bytes_accessed=0, transcendentals=0),
        name="logits",
    )(place, firsts, *chunks, *heads, *earlier)


def merge(mine, got):
    top = jnp.maximum(mine[:2], got[:2])
    sums = mine[2:] * jnp.exp(mine[:2] - top) + got[2:] * jnp.exp(got[:2] - top)
    return jnp.concatenate([top, sums], axis=0)


def grad_kernel(place, spots, turn, first, stats, local, targets, *refs):
    n = 2 * len(CALLS)
    e_hbm, heads, outs = refs[:n], refs[n : n + 2], refs[n + 2 : n + 8]
    g_own, g_other, u_keep, u_send, v_keep, v_send = refs[n + 8 : n + 14]
    canon, block, scales, e_all, w, sems = refs[n + 14 :]
    width = heads[0].shape[1]
    total = canon.shape[0]
    copies = []

    def copy(src, dst):
        copies.append(pltpu.make_async_copy(src, dst, sems.at[len(copies)]))
        copies[-1].start()
        return copies[-1]

    in_e, edge = [], [0]
    for i, e in enumerate(e_hbm):
        in_e.append(copy(e, e_all.at[i % 2, pl.ds(edge[-1], e.shape[0]), :]))
        if i % 2:
            edge.append(edge[-1] + e.shape[0])
    in_w = [copy(head, w.at[:, pl.ds(i * width, width)]) for i, head in enumerate(heads)]
    row = lax.broadcasted_iota(jnp.int32, (128, 128), 0)
    for i in range(8):
        tile = jnp.where(row == 2, targets[i : i + 1, :], 0.0)
        for j in (0, 1):
            scale = jnp.exp(local[j, i : i + 1, :] - stats[j, i : i + 1, :]) / stats[2 + j, i : i + 1, :]
            tile = jnp.where(row == j, (1.0 + j) * scale, tile)
        scales[i * 128 : (i + 1) * 128, :] = tile.T

    for call in range(len(CALLS)):
        in_e[2 * call].wait()
        in_e[2 * call + 1].wait()

        def rows16(i, _):
            here = pl.multiple_of(i * 16, 16)
            groups = [2 * i + k for k in (0, 1)]
            there = [pl.multiple_of(place[g] * GROUP, GROUP) for g in groups]
            s = jnp.concatenate(
                [scales[pl.ds(pl.multiple_of(spots[g] * GROUP, GROUP), GROUP), :] for g in groups], axis=0
            )
            target = s[:, 2:3].astype(jnp.int32)
            for half, out in ((0, g_own), (1, g_other)):
                cols = slice(half * width, (half + 1) * width)
                column = first[half] + lax.broadcasted_iota(jnp.int32, (16, width), 1)
                g = e_all[1, pl.ds(here, 16), cols] * s[:, 1:2] - e_all[0, pl.ds(here, 16), cols] * s[:, 0:1]
                g = jnp.where(target == column, g - 1.0, g)
                out[pl.ds(here, 16), :] = g.astype(BF16)
                for k in (0, 1):
                    canon[pl.ds(there[k], GROUP), cols] = g[k * GROUP : (k + 1) * GROUP, :]
            return 0

        lax.fori_loop(edge[call] // 16, edge[call + 1] // 16, rows16, 0, unroll=4)
    waits = [copy(g_own, outs[0]), copy(g_other, outs[1])]
    block[...] = canon[...].astype(BF16)
    for c in in_w:
        c.wait()

    wide, cut = u_keep.shape[-1], u_keep.shape[-2]
    for zb in (1, 0):
        for za in (1, 0):
            for x0 in (1, 0):
                where = pl.multiple_of(turn[x0 * 4 + zb * 2 + za] * wide, wide)
                r = lax.dot_general(
                    block[...], w[pl.ds(where, wide), :], (((1,), (1,)), ((), ())), preferred_element_type=F32
                ).reshape(2, 2, 2, total // 8, wide)
                for h in (0, 1):
                    x = x0 ^ h
                    for ya in (0, 1):
                        for yb in (0, 1):
                            low = r[h, yb, ya, :cut]
                            if zb == 0:
                                u_keep[yb, za, ya, h, x] = low
                            else:
                                u_send[yb, za, ya, h, x] = low.astype(BF16)
                        v_keep[zb, ya, za, x, h] = r[h, 0, ya, cut:]
                        v_send[zb, ya, za, x, h] = r[h, 1, ya, cut:].astype(BF16)
            pair = (u_send, outs[3]) if zb else (u_keep, outs[2])
            waits.append(copy(*(ref.at[:, za] for ref in pair)))
            for pair in ((v_keep, outs[4]), (v_send, outs[5])):
                waits.append(copy(*(ref.at[zb, :, za] for ref in pair)))
    for c in waits:
        c.wait()


def head_kernel(*refs):
    *rows, g, g_other, out = refs
    total, at = None, 0
    for r in rows:
        n = r.shape[0]
        lo = at % g.shape[0]
        part = (g if at < g.shape[0] else g_other)[lo : lo + n, :]
        product = lax.dot_general(r[...], part, (((0,), (0,)), ((), ())), preferred_element_type=F32)
        total = product if total is None else total + product
        at += n
    out[...] = total


def head_gradient(rows, g, g_other):
    ds, (total, width) = rows[0].shape[1], g.shape
    tile = 256
    whole = pl.BlockSpec(g.shape, lambda i: (0, 0))
    return pl.pallas_call(
        head_kernel,
        grid=(ds // tile,),
        out_shape=jax.ShapeDtypeStruct((ds, width), F32),
        in_specs=[pl.BlockSpec((r.shape[0], tile), lambda i: (0, i)) for r in rows] + [whole] * 2,
        out_specs=pl.BlockSpec((tile, width), lambda i: (i, 0)),
        compiler_params=pltpu.CompilerParams(vmem_limit_bytes=32 * 2**20),
        cost_estimate=pl.CostEstimate(flops=10**11, bytes_accessed=0, transcendentals=0),
        name="head",
    )(*rows, g, g_other)


def body(teacher_hidden, student_hidden, target_ids, teacher_head, student_head):
    dev = lax.axis_index("dp") * 8 + lax.axis_index("tensor")
    bit = bits_of(dev)
    width = teacher_head.shape[1]
    per = teacher_hidden.shape[0]
    dt, ds = teacher_hidden.shape[1], student_hidden.shape[1]

    ids = jnp.stack([target_ids // 256, target_ids % 256], axis=1).astype(BF16)
    own = jnp.concatenate([teacher_hidden, student_hidden, jnp.pad(ids, ((0, 0), (0, 126)))], axis=1)

    place, spots = [], []
    for call in CALLS:
        for i, late in call:
            first, n, slices, order = PARTS[i]
            half = n << (len(order) - 1)
            row = np.arange(late * half, (late + 1) * half, GROUP)
            rel = {d: (row // n >> k & 1).astype(np.int32) for k, d in enumerate(order)}
            if "Xa" in rel:
                a, b = rel["Xa"], rel["Xb"]
                rel["X1"] = a * (1 - bit["C"]) + b * bit["C"]
                rel["X0"] = b * (1 - bit["C"]) + a * bit["C"]
            (d,) = slices
            inner = first + (rel[d] ^ bit[d]) * n + (row % n).astype(np.int32)
            near = (rel["X1"] * 4 + rel["Yb"] * 2 + rel["Ya"]) * per
            fixed = ((rel["X1"] ^ bit["X1"]) * 4 + (rel["Yb"] ^ bit["Yb"]) * 2 + (rel["Ya"] ^ bit["Ya"])) * per
            place.append((near + inner) // GROUP)
            spots.append((fixed + inner) // GROUP)
    size = [sum(p.shape[0] for p in place[sum(map(len, CALLS[:k])) :][: len(call)]) for k, call in enumerate(CALLS)]
    place, spots = jnp.concatenate(place).astype(jnp.int32), jnp.concatenate(spots).astype(jnp.int32)
    spots_of = [spots[sum(size[:k]) : sum(size[: k + 1])] for k in range(len(CALLS))]
    turn = []
    for x0 in (0, 1):
        for zb in (0, 1):
            for za in (0, 1):
                xl = bit["X0"] ^ x0 ^ bit["X1"]
                z = z_of({"C": bit["C"], "Zb": bit["Zb"] ^ zb, "Za": bit["Za"] ^ za})
                turn.append(jnp.int32(xl * 4 + z))
    turn = jnp.stack(turn)
    firsts = jnp.stack([dev * width, (dev ^ 8) * width]).astype(jnp.int32)

    state = []
    for first, n, slices, _ in PARTS:
        index = 0
        for d in slices:
            index = index * 2 + bit[d]
        state.append([lax.dynamic_slice_in_dim(own, first + index * n, n, 0) if slices else own[first : first + n]])
    student_other, teacher_other = swap(student_head, "C"), swap(teacher_head, "C")
    for step in range(4):
        if step == 2:
            state, student_other, teacher_other = lax.optimization_barrier((state, student_other, teacher_other))
        elif step == 1:
            tables = (place, spots, spots_of, turn, firsts)
            state, tables = lax.optimization_barrier((state, tables))
            place, spots, spots_of, turn, firsts = tables
        elif step:
            state = lax.optimization_barrier(state)
        dims = [order[step] for *_, order in PARTS]
        for d in sorted(set(dims)):
            members = [i for i, other in enumerate(dims) if other == d]
            mine = [state[i][0] for i in members]
            got = swap(jnp.concatenate(mine, axis=0) if len(mine) > 1 else mine[0], d)
            at = 0
            for i, x in zip(members, mine):
                state[i] = [x, got[at : at + x.shape[0]] if len(mine) > 1 else got]
                at += x.shape[0]
                if step < 3:
                    state[i] = [jnp.concatenate(state[i], axis=0)]

    heads = (teacher_head, teacher_other, student_head, student_other)
    expos, rows, rows_other, side, at = [], [], [], (), 0
    for call, spots_here in zip(CALLS, spots_of):
        chunks = [state[i][late] for i, late in call]
        n = sum(x.shape[0] for x in chunks)
        e_t, e_s, r, *side = logits(chunks, spots_here, firsts, heads, per * 8, side)
        expos += [e_t, e_s]
        rows.append(r)
        at += n
    rows_other = [swap(r, "C") for r in rows]
    stats, targets = side
    local = stats
    for d in STAT_ORDER:
        stats = merge(stats, swap(stats, d))

    total, wide, cut = at, ds // 8, per // 2
    vmem = pl.BlockSpec(memory_space=pltpu.VMEM)
    smem = pl.BlockSpec(memory_space=pltpu.SMEM)
    shape = jax.ShapeDtypeStruct
    u, v = (2, 2, 2, 2, 2, cut, wide), (2, 2, 2, 2, 2, per - cut, wide)
    outs = [((total, width), BF16)] * 2 + [(u, F32), (u, BF16), (v, F32), (v, BF16)]
    far = pl.BlockSpec(memory_space=pl.ANY)
    g_own, g_other, u_keep, u_send, v_keep, v_send = pl.pallas_call(
        grad_kernel,
        out_shape=[shape(*o) for o in outs],
        in_specs=[smem] * 4 + [vmem] * 3 + [far] * (len(expos) + 2),
        out_specs=[far] * 6,
        scratch_shapes=[pltpu.VMEM(*o) for o in outs]
        + [
            pltpu.VMEM((total, 2 * width), F32),
            pltpu.VMEM((total, 2 * width), BF16),
            pltpu.VMEM((total, 128), F32),
            pltpu.VMEM((2, total, 2 * width), F32),
            pltpu.VMEM((ds, 2 * width), BF16),
            pltpu.SemaphoreType.DMA((len(expos) + 4 + 3 * 4,)),
        ],
        compiler_params=pltpu.CompilerParams(vmem_limit_bytes=56 * 2**20),
        name="grad",
    )(
        place, spots, turn, firsts, stats, local, targets, *expos, student_head, student_other
    )
    head_grad = head_gradient(rows + rows_other, g_own, swap(g_other, "C"))

    streams = [
        [u_keep, u_send, ("Zb", "Yb", "Za", "Ya", "X1", "X0")],
        [v_keep, v_send, ("Yb", "Zb", "Ya", "Za", "X0", "X1")],
    ]
    for step in range(6):
        back = [swap(s[1], s[2][step]) for s in streams]
        if step == 0:
            back[0], back[1], head_grad = lax.optimization_barrier((back[0], back[1], head_grad))
        for s, got in zip(streams, back):
            new = s[0] + got.astype(F32)
            if step == 5:
                s[0] = new
                continue
            s[0], send = new[0], new[1]
            s[1] = send.astype(BF16) if step + 1 < NARROW_STEPS else send
    input_grad = jnp.concatenate([s[0] for s in streams], axis=0)
    return (head_grad, input_grad)


def solution(mesh):
    placed = (
        P("dp", None),
        P("dp", None),
        P("dp"),
        P(None, ("dp", "tensor")),
        P(None, ("dp", "tensor")),
    )
    return jax.shard_map(
        body,
        mesh=mesh,
        in_specs=placed,
        out_specs=(P(None, ("dp", "tensor")), P("dp", "tensor")),
        check_vma=False,
    )
```

```python
import functools

import jax
import jax.numpy as jnp
import numpy as np
from jax import lax
from jax.experimental import pallas as pl
from jax.experimental.pallas import tpu as pltpu
from jax.sharding import PartitionSpec as P

VOCAB = 64128
F32, BF16 = jnp.float32, jnp.bfloat16
AXES = ("dp", "tensor")

PARTS = (
    (0, 24, ("Zb",), ("X1", "Ya", "Zb", "Yb")),
    (48, 24, ("X0",), ("Yb", "Ya", "Xa", "Xb")),
    (96, 16, ("Za",), ("Yb", "X1", "Ya", "Za")),
)
CALLS = (((0, 0), (1, 0), (2, 0)), ((2, 1),), ((0, 1), (1, 1)))
STAT_ORDER = ("Ya", "Za", "X0", "X1", "Zb", "Yb")
NARROW_STEPS = 4
GROUP = 8
TALL = 32
SLAB = 1024


def bits_of(dev):
    dp, tensor = dev // 8, dev % 8
    xh, y, core = dp // 8, (dp // 2) % 4, dp % 2
    xl, z = tensor // 4, tensor % 4
    gx, gy, gz = xh * 2 + (xh ^ xl), y ^ (y // 2), z ^ (z // 2)
    pick = lambda g, second: (g // 2) * second + (g % 2) * (1 - second)
    return {
        "X1": xh, "X0": xh ^ xl,
        "Xa": pick(gx, 1 - core), "Xb": pick(gx, core),
        "Ya": pick(gy, core), "Yb": pick(gy, 1 - core),
        "Za": pick(gz, core), "Zb": pick(gz, 1 - core),
        "C": core,
    }


def z_of(bits):
    core = bits["C"]
    high = bits["Zb"] * (1 - core) + bits["Za"] * core
    low = bits["Za"] * (1 - core) + bits["Zb"] * core
    return high * 2 + (high ^ low)


@functools.cache
def pairs(dim):
    if dim == "C":
        return [(d, d ^ 8) for d in range(128)]
    basis = ("X1", "X0", "Ya", "Yb", "Za", "Zb", "C")
    key = lambda b: tuple(b[k] for k in basis)
    table = {key(bits_of(d)): d for d in range(128)}
    out = []
    for d in range(128):
        b = bits_of(d)
        real = dim
        if dim in ("Xa", "Xb"):
            real = "X1" if (dim == "Xa") == (b["C"] == 0) else "X0"
        out.append((d, table[key(dict(b, **{real: 1 - b[real]}))]))
    return out


def swap(x, dim):
    return lax.ppermute(x, AXES, pairs(dim))


def logits_kernel(counts, last, place, first, *refs):
    n = len(counts)
    x_refs = refs[:n]
    heads = refs[n : n + 4]
    earlier = refs[n + 4 : n + 6]
    e_t, e_s, rows_out, stats, targets, canon, lines, x, w_t, w_s, z_t, z_s, sems = refs[n + 4 + 2 * last :]
    dt, ds, width = w_t.shape[0], w_s.shape[0], heads[0].shape[1]
    total = sum(counts)
    copies = []

    def copy(src, dst):
        copies.append(pltpu.make_async_copy(src, dst, sems.at[len(copies)]))
        copies[-1].start()
        return copies[-1]

    def rows_in(cols):
        out, at = [], 0
        for ref, count in zip(x_refs, counts):
            out.append(copy(ref.at[:, cols], x.at[pl.ds(at, count), cols]))
            at += count
        return out

    def slabs_in(own, other, w, depth):
        return [
            [
                copy(head.at[pl.ds(lo, SLAB), :], w.at[pl.ds(lo, SLAB), pl.ds(half * width, width)])
                for half, head in enumerate((own, other))
            ]
            for lo in range(0, depth, SLAB)
        ]

    x_s = rows_in(pl.ds(dt, x.shape[1] - dt))
    in_s = slabs_in(heads[2], heads[3], w_s, ds)
    x_t = rows_in(pl.ds(0, dt))
    in_t = slabs_in(heads[0], heads[1], w_t, dt)
    outs = []
    canon[...] = jnp.zeros_like(canon)
    lane = lax.broadcasted_iota(jnp.int32, (TALL, 128), 1)
    lane_width = lax.broadcasted_iota(jnp.int32, (1, width), 1)
    real = jnp.concatenate([first[half] + lane_width < VOCAB for half in (0, 1)], axis=1)

    def products(arrived, lo, w, z):
        for k, slab in enumerate(arrived):
            for c in slab:
                c.wait()
            for left in range(0, 2 * width, 256):
                r = jnp.dot(
                    x[:, lo + k * SLAB : lo + (k + 1) * SLAB],
                    w[k * SLAB : (k + 1) * SLAB, left : left + 256],
                    preferred_element_type=F32,
                )
                z[:, left : left + 256] = r if k == 0 else z[:, left : left + 256] + r

    def exponentials(z, rows):
        value = jnp.where(real, z[rows, :], F32(-1e30))
        top = jnp.max(value, axis=1, keepdims=True)
        e = jnp.exp(value - top)
        z[rows, :] = e
        return top, jnp.sum(e, axis=1, keepdims=True)

    for c in x_s:
        c.wait()
    outs.append(copy(x.at[:, pl.ds(dt, ds)], rows_out))
    products(in_s, dt, w_s, z_s)
    for lo in range(0, total, TALL):
        rows = slice(lo, lo + TALL)
        digits = x[rows, dt + ds :].astype(F32)
        m_s, n_s = exponentials(z_s, rows)
        line = jnp.where(lane == 1, m_s, 0.0)
        line = jnp.where(lane == 3, n_s, line)
        lines[rows, :] = jnp.where(lane == 4, digits[:, 0:1] * 256.0 + digits[:, 1:2], line)
    outs.append(copy(z_s, e_s))
    for c in x_t:
        c.wait()
    products(in_t, 0, w_t, z_t)
    for lo in range(0, total, TALL):
        rows = slice(lo, lo + TALL)
        m_t, n_t = exponentials(z_t, rows)
        line = jnp.where(lane == 0, m_t, lines[rows, :])
        line = jnp.where(lane == 2, n_t, line)
        for k in range(0, TALL, GROUP):
            spot = pl.multiple_of(place[(lo + k) // GROUP] * GROUP, GROUP)
            canon[pl.ds(spot, GROUP), :] = line[k : k + GROUP, :]
        if (lo + TALL) % 128 == 0:
            part = pl.ds(lo + TALL - 128, 128)
            outs.append(copy(z_t.at[part, :], e_t.at[part, :]))
    for i in range(8):
        across = canon[i * 128 : (i + 1) * 128, :].T
        for j in range(5):
            out, old = (stats.at[j], earlier[0].at[j] if last else None) if j < 4 else (targets, earlier[1] if last else None)
            value = across[j : j + 1, :]
            out[i : i + 1, :] = value + old[i : i + 1, :] if last else value
    for c in outs:
        c.wait()


def logits(chunks, place, firsts, heads, rows, earlier):
    counts = tuple(x.shape[0] for x in chunks)
    total = sum(counts)
    dt, (ds, width) = heads[0].shape[0], heads[2].shape
    shape = jax.ShapeDtypeStruct
    smem, vmem, far = (pl.BlockSpec(memory_space=m) for m in (pltpu.SMEM, pltpu.VMEM, pl.ANY))
    n_copies = 2 * len(chunks) + 2 * (dt + ds) // SLAB + 2 + total // 128
    return pl.pallas_call(
        functools.partial(logits_kernel, counts, bool(earlier)),
        out_shape=[
            shape((total, 2 * width), F32), shape((total, 2 * width), F32), shape((total, ds), BF16),
            shape((4, 8, 128), F32), shape((8, 128), F32),
        ],
        in_specs=[smem] * 2 + [far] * (len(chunks) + 4) + [vmem] * len(earlier),
        out_specs=[far] * 3 + [vmem] * 2,
        scratch_shapes=[
            pltpu.VMEM((rows, 128), F32),
            pltpu.VMEM((total, 128), F32),
            pltpu.VMEM((total, chunks[0].shape[1]), BF16),
            pltpu.VMEM((dt, 2 * width), BF16),
            pltpu.VMEM((ds, 2 * width), BF16),
            pltpu.VMEM((total, 2 * width), F32),
            pltpu.VMEM((total, 2 * width), F32),
            pltpu.SemaphoreType.DMA((n_copies,)),
        ],
        compiler_params=pltpu.CompilerParams(vmem_limit_bytes=56 * 2**20),
        cost_estimate=pl.CostEstimate(flops=10**11, bytes_accessed=0, transcendentals=0),
        name="logits",
    )(place, firsts, *chunks, *heads, *earlier)


def merge(mine, got):
    top = jnp.maximum(mine[:2], got[:2])
    sums = mine[2:] * jnp.exp(mine[:2] - top) + got[2:] * jnp.exp(got[:2] - top)
    return jnp.concatenate([top, sums], axis=0)


def grad_kernel(place, spots, turn, first, stats, local, targets, *refs):
    n = 2 * len(CALLS)
    e_hbm, heads, outs = refs[:n], refs[n : n + 2], refs[n + 2 : n + 8]
    g_own, g_other, u_keep, u_send, v_keep, v_send = refs[n + 8 : n + 14]
    canon, block, scales, e_all, w, sems = refs[n + 14 :]
    width = heads[0].shape[1]
    total = canon.shape[0]
    copies = []

    def copy(src, dst):
        copies.append(pltpu.make_async_copy(src, dst, sems.at[len(copies)]))
        copies[-1].start()
        return copies[-1]

    in_e, edge = [], [0]
    for i, e in enumerate(e_hbm):
        in_e.append(copy(e, e_all.at[i % 2, pl.ds(edge[-1], e.shape[0]), :]))
        if i % 2:
            edge.append(edge[-1] + e.shape[0])
    in_w = [copy(head, w.at[:, pl.ds(i * width, width)]) for i, head in enumerate(heads)]
    row = lax.broadcasted_iota(jnp.int32, (128, 128), 0)
    for i in range(8):
        tile = jnp.where(row == 2, targets[i : i + 1, :], 0.0)
        for j in (0, 1):
            scale = jnp.exp(local[j, i : i + 1, :] - stats[j, i : i + 1, :]) / stats[2 + j, i : i + 1, :]
            tile = jnp.where(row == j, (1.0 + j) * scale, tile)
        scales[i * 128 : (i + 1) * 128, :] = tile.T

    for call in range(len(CALLS)):
        in_e[2 * call].wait()
        in_e[2 * call + 1].wait()

        def rows16(i, _):
            here = pl.multiple_of(i * 16, 16)
            groups = [2 * i + k for k in (0, 1)]
            there = [pl.multiple_of(place[g] * GROUP, GROUP) for g in groups]
            s = jnp.concatenate(
                [scales[pl.ds(pl.multiple_of(spots[g] * GROUP, GROUP), GROUP), :] for g in groups], axis=0
            )
            target = s[:, 2:3].astype(jnp.int32)
            for half, out in ((0, g_own), (1, g_other)):
                cols = slice(half * width, (half + 1) * width)
                column = first[half] + lax.broadcasted_iota(jnp.int32, (16, width), 1)
                g = e_all[1, pl.ds(here, 16), cols] * s[:, 1:2] - e_all[0, pl.ds(here, 16), cols] * s[:, 0:1]
                g = jnp.where(target == column, g - 1.0, g)
                out[pl.ds(here, 16), :] = g.astype(BF16)
                for k in (0, 1):
                    canon[pl.ds(there[k], GROUP), cols] = g[k * GROUP : (k + 1) * GROUP, :]
            return 0

        lax.fori_loop(edge[call] // 16, edge[call + 1] // 16, rows16, 0, unroll=4)
    waits = [copy(g_own, outs[0]), copy(g_other, outs[1])]
    block[...] = canon[...].astype(BF16)
    for c in in_w:
        c.wait()

    wide, cut = u_keep.shape[-1], u_keep.shape[-2]
    for zb in (1, 0):
        for za in (1, 0):
            for x0 in (1, 0):
                where = pl.multiple_of(turn[x0 * 4 + zb * 2 + za] * wide, wide)
                r = lax.dot_general(
                    block[...], w[pl.ds(where, wide), :], (((1,), (1,)), ((), ())), preferred_element_type=F32
                ).reshape(2, 2, 2, total // 8, wide)
                for h in (0, 1):
                    x = x0 ^ h
                    for ya in (0, 1):
                        for yb in (0, 1):
                            low = r[h, yb, ya, :cut]
                            if zb == 0:
                                u_keep[yb, za, ya, h, x] = low
                            else:
                                u_send[yb, za, ya, h, x] = low.astype(BF16)
                        v_keep[zb, ya, za, x, h] = r[h, 0, ya, cut:]
                        v_send[zb, ya, za, x, h] = r[h, 1, ya, cut:].astype(BF16)
            pair = (u_send, outs[3]) if zb else (u_keep, outs[2])
            waits.append(copy(*(ref.at[:, za] for ref in pair)))
            for pair in ((v_keep, outs[4]), (v_send, outs[5])):
                waits.append(copy(*(ref.at[zb, :, za] for ref in pair)))
    for c in waits:
        c.wait()


def head_kernel(*refs):
    *rows, g, g_other, out = refs
    total, at = None, 0
    for r in rows:
        n = r.shape[0]
        lo = at % g.shape[0]
        part = (g if at < g.shape[0] else g_other)[lo : lo + n, :]
        product = lax.dot_general(r[...], part, (((0,), (0,)), ((), ())), preferred_element_type=F32)
        total = product if total is None else total + product
        at += n
    out[...] = total


def head_gradient(rows, g, g_other):
    ds, (total, width) = rows[0].shape[1], g.shape
    tile = 256
    whole = pl.BlockSpec(g.shape, lambda i: (0, 0))
    return pl.pallas_call(
        head_kernel,
        grid=(ds // tile,),
        out_shape=jax.ShapeDtypeStruct((ds, width), F32),
        in_specs=[pl.BlockSpec((r.shape[0], tile), lambda i: (0, i)) for r in rows] + [whole] * 2,
        out_specs=pl.BlockSpec((tile, width), lambda i: (i, 0)),
        compiler_params=pltpu.CompilerParams(vmem_limit_bytes=32 * 2**20),
        cost_estimate=pl.CostEstimate(flops=10**11, bytes_accessed=0, transcendentals=0),
        name="head",
    )(*rows, g, g_other)


def body(teacher_hidden, student_hidden, target_ids, teacher_head, student_head):
    dev = lax.axis_index("dp") * 8 + lax.axis_index("tensor")
    bit = bits_of(dev)
    width = teacher_head.shape[1]
    per = teacher_hidden.shape[0]
    dt, ds = teacher_hidden.shape[1], student_hidden.shape[1]

    ids = jnp.stack([target_ids // 256, target_ids % 256], axis=1).astype(BF16)
    own = jnp.concatenate([teacher_hidden, student_hidden, jnp.pad(ids, ((0, 0), (0, 126)))], axis=1)

    place, spots = [], []
    for call in CALLS:
        for i, late in call:
            first, n, slices, order = PARTS[i]
            half = n << (len(order) - 1)
            row = np.arange(late * half, (late + 1) * half, GROUP)
            rel = {d: (row // n >> k & 1).astype(np.int32) for k, d in enumerate(order)}
            if "Xa" in rel:
                a, b = rel["Xa"], rel["Xb"]
                rel["X1"] = a * (1 - bit["C"]) + b * bit["C"]
                rel["X0"] = b * (1 - bit["C"]) + a * bit["C"]
            (d,) = slices
            inner = first + (rel[d] ^ bit[d]) * n + (row % n).astype(np.int32)
            near = (rel["X1"] * 4 + rel["Yb"] * 2 + rel["Ya"]) * per
            fixed = ((rel["X1"] ^ bit["X1"]) * 4 + (rel["Yb"] ^ bit["Yb"]) * 2 + (rel["Ya"] ^ bit["Ya"])) * per
            place.append((near + inner) // GROUP)
            spots.append((fixed + inner) // GROUP)
    size = [sum(p.shape[0] for p in place[sum(map(len, CALLS[:k])) :][: len(call)]) for k, call in enumerate(CALLS)]
    place, spots = jnp.concatenate(place).astype(jnp.int32), jnp.concatenate(spots).astype(jnp.int32)
    spots_of = [spots[sum(size[:k]) : sum(size[: k + 1])] for k in range(len(CALLS))]
    turn = []
    for x0 in (0, 1):
        for zb in (0, 1):
            for za in (0, 1):
                xl = bit["X0"] ^ x0 ^ bit["X1"]
                z = z_of({"C": bit["C"], "Zb": bit["Zb"] ^ zb, "Za": bit["Za"] ^ za})
                turn.append(jnp.int32(xl * 4 + z))
    turn = jnp.stack(turn)
    firsts = jnp.stack([dev * width, (dev ^ 8) * width]).astype(jnp.int32)

    state = []
    for first, n, slices, _ in PARTS:
        index = 0
        for d in slices:
            index = index * 2 + bit[d]
        state.append([lax.dynamic_slice_in_dim(own, first + index * n, n, 0) if slices else own[first : first + n]])
    student_other, teacher_other = swap(student_head, "C"), swap(teacher_head, "C")
    for step in range(3):
        if step == 2:
            state, student_other, teacher_other = lax.optimization_barrier((state, student_other, teacher_other))
        elif step == 1:
            tables = (place, spots, spots_of, turn, firsts)
            state, tables = lax.optimization_barrier((state, tables))
            place, spots, spots_of, turn, firsts = tables
        dims = [order[step] for *_, order in PARTS]
        for d in sorted(set(dims)):
            members = [i for i, other in enumerate(dims) if other == d]
            mine = [state[i][0] for i in members]
            got = swap(jnp.concatenate(mine, axis=0) if len(mine) > 1 else mine[0], d)
            at = 0
            for i, x in zip(members, mine):
                state[i] = [x, got[at : at + x.shape[0]] if len(mine) > 1 else got]
                at += x.shape[0]
                if step < 2:
                    state[i] = [jnp.concatenate(state[i], axis=0)]
    state = [(early, [swap(x, order[3]) for x in early]) for early, (*_, order) in zip(state, PARTS)]

    heads = (teacher_head, teacher_other, student_head, student_other)
    expos, rows, rows_other, side, at = [], [], [], (), 0
    for call, spots_here in zip(CALLS, spots_of):
        chunks = [x for i, late in call for x in state[i][late]]
        n = sum(x.shape[0] for x in chunks)
        e_t, e_s, r, *side = logits(chunks, spots_here, firsts, heads, per * 8, side)
        expos += [e_t, e_s]
        rows.append(r)
        at += n
    rows_other = [swap(r, "C") for r in rows]
    stats, targets = side
    local = stats
    for d in STAT_ORDER:
        stats = merge(stats, swap(stats, d))

    total, wide, cut = at, ds // 8, per // 2
    vmem = pl.BlockSpec(memory_space=pltpu.VMEM)
    smem = pl.BlockSpec(memory_space=pltpu.SMEM)
    shape = jax.ShapeDtypeStruct
    u, v = (2, 2, 2, 2, 2, cut, wide), (2, 2, 2, 2, 2, per - cut, wide)
    outs = [((total, width), BF16)] * 2 + [(u, F32), (u, BF16), (v, F32), (v, BF16)]
    far = pl.BlockSpec(memory_space=pl.ANY)
    g_own, g_other, u_keep, u_send, v_keep, v_send = pl.pallas_call(
        grad_kernel,
        out_shape=[shape(*o) for o in outs],
        in_specs=[smem] * 4 + [vmem] * 3 + [far] * (len(expos) + 2),
        out_specs=[far] * 6,
        scratch_shapes=[pltpu.VMEM(*o) for o in outs]
        + [
            pltpu.VMEM((total, 2 * width), F32),
            pltpu.VMEM((total, 2 * width), BF16),
            pltpu.VMEM((total, 128), F32),
            pltpu.VMEM((2, total, 2 * width), F32),
            pltpu.VMEM((ds, 2 * width), BF16),
            pltpu.SemaphoreType.DMA((len(expos) + 4 + 3 * 4,)),
        ],
        compiler_params=pltpu.CompilerParams(vmem_limit_bytes=56 * 2**20),
        name="grad",
    )(
        place, spots, turn, firsts, stats, local, targets, *expos, student_head, student_other
    )
    head_grad = head_gradient(rows + rows_other, g_own, swap(g_other, "C"))

    streams = [
        [u_keep, u_send, ("Zb", "Yb", "Za", "Ya", "X1", "X0")],
        [v_keep, v_send, ("Yb", "Zb", "Ya", "Za", "X0", "X1")],
    ]
    for step in range(6):
        back = [swap(s[1], s[2][step]) for s in streams]
        if step == 0:
            back[0], back[1], head_grad = lax.optimization_barrier((back[0], back[1], head_grad))
        for s, got in zip(streams, back):
            new = s[0] + got.astype(F32)
            if step == 5:
                s[0] = new
                continue
            s[0], send = new[0], new[1]
            s[1] = send.astype(BF16) if step + 1 < NARROW_STEPS else send
    input_grad = jnp.concatenate([s[0] for s in streams], axis=0)
    return (head_grad, input_grad)


def solution(mesh):
    placed = (
        P("dp", None),
        P("dp", None),
        P("dp"),
        P(None, ("dp", "tensor")),
        P(None, ("dp", "tensor")),
    )
    return jax.shard_map(
        body,
        mesh=mesh,
        in_specs=placed,
        out_specs=(P(None, ("dp", "tensor")), P("dp", "tensor")),
        check_vma=False,
    )
```

```python
import functools

import jax
import jax.numpy as jnp
import numpy as np
from jax import lax
from jax.experimental import pallas as pl
from jax.experimental.pallas import tpu as pltpu
from jax.sharding import PartitionSpec as P

VOCAB = 64128
F32, BF16 = jnp.float32, jnp.bfloat16
AXES = ("dp", "tensor")

PARTS = (
    (0, 24, ("Zb",), ("X1", "Ya", "Zb", "Yb")),
    (48, 24, ("X0",), ("Yb", "Ya", "Xa", "Xb")),
    (96, 16, ("Za",), ("Yb", "X1", "Ya", "Za")),
)
EARLY = (0, 1)
CALLS = (((0, 0), (1, 0), (2, 0)), ((2, 1),), ((0, 1), (1, 1)))
STAT_ORDER = ("Ya", "Za", "X0", "X1", "Zb", "Yb")
NARROW_STEPS = 4
GROUP = 8
TALL = 32
SLAB = 1024


def bits_of(dev):
    dp, tensor = dev // 8, dev % 8
    xh, y, core = dp // 8, (dp // 2) % 4, dp % 2
    xl, z = tensor // 4, tensor % 4
    gx, gy, gz = xh * 2 + (xh ^ xl), y ^ (y // 2), z ^ (z // 2)
    pick = lambda g, second: (g // 2) * second + (g % 2) * (1 - second)
    return {
        "X1": xh, "X0": xh ^ xl,
        "Xa": pick(gx, 1 - core), "Xb": pick(gx, core),
        "Ya": pick(gy, core), "Yb": pick(gy, 1 - core),
        "Za": pick(gz, core), "Zb": pick(gz, 1 - core),
        "C": core,
    }


def z_of(bits):
    core = bits["C"]
    high = bits["Zb"] * (1 - core) + bits["Za"] * core
    low = bits["Za"] * (1 - core) + bits["Zb"] * core
    return high * 2 + (high ^ low)


@functools.cache
def pairs(dim):
    if dim == "C":
        return [(d, d ^ 8) for d in range(128)]
    basis = ("X1", "X0", "Ya", "Yb", "Za", "Zb", "C")
    key = lambda b: tuple(b[k] for k in basis)
    table = {key(bits_of(d)): d for d in range(128)}
    out = []
    for d in range(128):
        b = bits_of(d)
        real = dim
        if dim in ("Xa", "Xb"):
            real = "X1" if (dim == "Xa") == (b["C"] == 0) else "X0"
        out.append((d, table[key(dict(b, **{real: 1 - b[real]}))]))
    return out


def swap(x, dim):
    return lax.ppermute(x, AXES, pairs(dim))


def logits_kernel(counts, last, place, first, *refs):
    n = len(counts)
    x_refs = refs[:n]
    heads = refs[n : n + 4]
    earlier = refs[n + 4 : n + 6]
    e_t, e_s, rows_out, stats, targets, canon, lines, x, w_t, w_s, z_t, z_s, sems = refs[n + 4 + 2 * last :]
    dt, ds, width = w_t.shape[0], w_s.shape[0], heads[0].shape[1]
    total = sum(counts)
    copies = []

    def copy(src, dst):
        copies.append(pltpu.make_async_copy(src, dst, sems.at[len(copies)]))
        copies[-1].start()
        return copies[-1]

    def rows_in(cols):
        out, at = [], 0
        for ref, count in zip(x_refs, counts):
            out.append(copy(ref.at[:, cols], x.at[pl.ds(at, count), cols]))
            at += count
        return out

    def slabs_in(own, other, w, depth):
        return [
            [
                copy(head.at[pl.ds(lo, SLAB), :], w.at[pl.ds(lo, SLAB), pl.ds(half * width, width)])
                for half, head in enumerate((own, other))
            ]
            for lo in range(0, depth, SLAB)
        ]

    x_s = rows_in(pl.ds(dt, x.shape[1] - dt))
    in_s = slabs_in(heads[2], heads[3], w_s, ds)
    x_t = rows_in(pl.ds(0, dt))
    in_t = slabs_in(heads[0], heads[1], w_t, dt)
    outs = []
    canon[...] = jnp.zeros_like(canon)
    lane = lax.broadcasted_iota(jnp.int32, (TALL, 128), 1)
    lane_width = lax.broadcasted_iota(jnp.int32, (1, width), 1)
    real = jnp.concatenate([first[half] + lane_width < VOCAB for half in (0, 1)], axis=1)

    def products(arrived, lo, w, z):
        for k, slab in enumerate(arrived):
            for c in slab:
                c.wait()
            for left in range(0, 2 * width, 256):
                r = jnp.dot(
                    x[:, lo + k * SLAB : lo + (k + 1) * SLAB],
                    w[k * SLAB : (k + 1) * SLAB, left : left + 256],
                    preferred_element_type=F32,
                )
                z[:, left : left + 256] = r if k == 0 else z[:, left : left + 256] + r

    def exponentials(z, rows):
        value = jnp.where(real, z[rows, :], F32(-1e30))
        top = jnp.max(value, axis=1, keepdims=True)
        e = jnp.exp(value - top)
        z[rows, :] = e
        return top, jnp.sum(e, axis=1, keepdims=True)

    for c in x_s:
        c.wait()
    outs.append(copy(x.at[:, pl.ds(dt, ds)], rows_out))
    products(in_s, dt, w_s, z_s)
    for lo in range(0, total, TALL):
        rows = slice(lo, lo + TALL)
        digits = x[rows, dt + ds :].astype(F32)
        m_s, n_s = exponentials(z_s, rows)
        line = jnp.where(lane == 1, m_s, 0.0)
        line = jnp.where(lane == 3, n_s, line)
        lines[rows, :] = jnp.where(lane == 4, digits[:, 0:1] * 256.0 + digits[:, 1:2], line)
    outs.append(copy(z_s, e_s))
    for c in x_t:
        c.wait()
    products(in_t, 0, w_t, z_t)
    for lo in range(0, total, TALL):
        rows = slice(lo, lo + TALL)
        m_t, n_t = exponentials(z_t, rows)
        line = jnp.where(lane == 0, m_t, lines[rows, :])
        line = jnp.where(lane == 2, n_t, line)
        for k in range(0, TALL, GROUP):
            spot = pl.multiple_of(place[(lo + k) // GROUP] * GROUP, GROUP)
            canon[pl.ds(spot, GROUP), :] = line[k : k + GROUP, :]
        if (lo + TALL) % 128 == 0:
            part = pl.ds(lo + TALL - 128, 128)
            outs.append(copy(z_t.at[part, :], e_t.at[part, :]))
    for i in range(8):
        across = canon[i * 128 : (i + 1) * 128, :].T
        for j in range(5):
            out, old = (stats.at[j], earlier[0].at[j] if last else None) if j < 4 else (targets, earlier[1] if last else None)
            value = across[j : j + 1, :]
            out[i : i + 1, :] = value + old[i : i + 1, :] if last else value
    for c in outs:
        c.wait()


def logits(chunks, place, firsts, heads, rows, earlier):
    counts = tuple(x.shape[0] for x in chunks)
    total = sum(counts)
    dt, (ds, width) = heads[0].shape[0], heads[2].shape
    shape = jax.ShapeDtypeStruct
    smem, vmem, far = (pl.BlockSpec(memory_space=m) for m in (pltpu.SMEM, pltpu.VMEM, pl.ANY))
    n_copies = 2 * len(chunks) + 2 * (dt + ds) // SLAB + 2 + total // 128
    return pl.pallas_call(
        functools.partial(logits_kernel, counts, bool(earlier)),
        out_shape=[
            shape((total, 2 * width), F32), shape((total, 2 * width), F32), shape((total, ds), BF16),
            shape((4, 8, 128), F32), shape((8, 128), F32),
        ],
        in_specs=[smem] * 2 + [far] * (len(chunks) + 4) + [vmem] * len(earlier),
        out_specs=[far] * 3 + [vmem] * 2,
        scratch_shapes=[
            pltpu.VMEM((rows, 128), F32),
            pltpu.VMEM((total, 128), F32),
            pltpu.VMEM((total, chunks[0].shape[1]), BF16),
            pltpu.VMEM((dt, 2 * width), BF16),
            pltpu.VMEM((ds, 2 * width), BF16),
            pltpu.VMEM((total, 2 * width), F32),
            pltpu.VMEM((total, 2 * width), F32),
            pltpu.SemaphoreType.DMA((n_copies,)),
        ],
        compiler_params=pltpu.CompilerParams(vmem_limit_bytes=56 * 2**20),
        cost_estimate=pl.CostEstimate(flops=10**11, bytes_accessed=0, transcendentals=0),
        name="logits",
    )(place, firsts, *chunks, *heads, *earlier)


def merge(mine, got):
    top = jnp.maximum(mine[:2], got[:2])
    sums = mine[2:] * jnp.exp(mine[:2] - top) + got[2:] * jnp.exp(got[:2] - top)
    return jnp.concatenate([top, sums], axis=0)


def grad_kernel(place, spots, turn, first, stats, local, targets, *refs):
    n = 2 * len(CALLS)
    e_hbm, heads, outs = refs[:n], refs[n : n + 2], refs[n + 2 : n + 8]
    g_own, g_other, u_keep, u_send, v_keep, v_send = refs[n + 8 : n + 14]
    canon, block, scales, e_all, w, sems = refs[n + 14 :]
    width = heads[0].shape[1]
    total = canon.shape[0]
    copies = []

    def copy(src, dst):
        copies.append(pltpu.make_async_copy(src, dst, sems.at[len(copies)]))
        copies[-1].start()
        return copies[-1]

    in_e, edge = [], [0]
    for i, e in enumerate(e_hbm):
        in_e.append(copy(e, e_all.at[i % 2, pl.ds(edge[-1], e.shape[0]), :]))
        if i % 2:
            edge.append(edge[-1] + e.shape[0])
    in_w = [copy(head, w.at[:, pl.ds(i * width, width)]) for i, head in enumerate(heads)]
    row = lax.broadcasted_iota(jnp.int32, (128, 128), 0)
    for i in range(8):
        tile = jnp.where(row == 2, targets[i : i + 1, :], 0.0)
        for j in (0, 1):
            scale = jnp.exp(local[j, i : i + 1, :] - stats[j, i : i + 1, :]) / stats[2 + j, i : i + 1, :]
            tile = jnp.where(row == j, (1.0 + j) * scale, tile)
        scales[i * 128 : (i + 1) * 128, :] = tile.T

    for call in range(len(CALLS)):
        in_e[2 * call].wait()
        in_e[2 * call + 1].wait()

        def rows16(i, _):
            here = pl.multiple_of(i * 16, 16)
            groups = [2 * i + k for k in (0, 1)]
            there = [pl.multiple_of(place[g] * GROUP, GROUP) for g in groups]
            s = jnp.concatenate(
                [scales[pl.ds(pl.multiple_of(spots[g] * GROUP, GROUP), GROUP), :] for g in groups], axis=0
            )
            target = s[:, 2:3].astype(jnp.int32)
            for half, out in ((0, g_own), (1, g_other)):
                cols = slice(half * width, (half + 1) * width)
                column = first[half] + lax.broadcasted_iota(jnp.int32, (16, width), 1)
                g = e_all[1, pl.ds(here, 16), cols] * s[:, 1:2] - e_all[0, pl.ds(here, 16), cols] * s[:, 0:1]
                g = jnp.where(target == column, g - 1.0, g)
                out[pl.ds(here, 16), :] = g.astype(BF16)
                for k in (0, 1):
                    canon[pl.ds(there[k], GROUP), cols] = g[k * GROUP : (k + 1) * GROUP, :]
            return 0

        lax.fori_loop(edge[call] // 16, edge[call + 1] // 16, rows16, 0, unroll=4)
    waits = [copy(g_own, outs[0]), copy(g_other, outs[1])]
    block[...] = canon[...].astype(BF16)
    for c in in_w:
        c.wait()

    wide, cut = u_keep.shape[-1], u_keep.shape[-2]
    for zb in (1, 0):
        for za in (1, 0):
            for x0 in (1, 0):
                where = pl.multiple_of(turn[x0 * 4 + zb * 2 + za] * wide, wide)
                r = lax.dot_general(
                    block[...], w[pl.ds(where, wide), :], (((1,), (1,)), ((), ())), preferred_element_type=F32
                ).reshape(2, 2, 2, total // 8, wide)
                for h in (0, 1):
                    x = x0 ^ h
                    for ya in (0, 1):
                        for yb in (0, 1):
                            low = r[h, yb, ya, :cut]
                            if zb == 0:
                                u_keep[yb, za, ya, h, x] = low
                            else:
                                u_send[yb, za, ya, h, x] = low.astype(BF16)
                        v_keep[zb, ya, za, x, h] = r[h, 0, ya, cut:]
                        v_send[zb, ya, za, x, h] = r[h, 1, ya, cut:].astype(BF16)
            pair = (u_send, outs[3]) if zb else (u_keep, outs[2])
            waits.append(copy(*(ref.at[:, za] for ref in pair)))
            for pair in ((v_keep, outs[4]), (v_send, outs[5])):
                waits.append(copy(*(ref.at[zb, :, za] for ref in pair)))
    for c in waits:
        c.wait()


def head_kernel(*refs):
    *rows, g, g_other, out = refs
    total, at = None, 0
    for r in rows:
        n = r.shape[0]
        lo = at % g.shape[0]
        part = (g if at < g.shape[0] else g_other)[lo : lo + n, :]
        product = lax.dot_general(r[...], part, (((0,), (0,)), ((), ())), preferred_element_type=F32)
        total = product if total is None else total + product
        at += n
    out[...] = total


def head_gradient(rows, g, g_other):
    ds, (total, width) = rows[0].shape[1], g.shape
    tile = 256
    whole = pl.BlockSpec(g.shape, lambda i: (0, 0))
    return pl.pallas_call(
        head_kernel,
        grid=(ds // tile,),
        out_shape=jax.ShapeDtypeStruct((ds, width), F32),
        in_specs=[pl.BlockSpec((r.shape[0], tile), lambda i: (0, i)) for r in rows] + [whole] * 2,
        out_specs=pl.BlockSpec((tile, width), lambda i: (i, 0)),
        compiler_params=pltpu.CompilerParams(vmem_limit_bytes=32 * 2**20),
        cost_estimate=pl.CostEstimate(flops=10**11, bytes_accessed=0, transcendentals=0),
        name="head",
    )(*rows, g, g_other)


def body(teacher_hidden, student_hidden, target_ids, teacher_head, student_head):
    dev = lax.axis_index("dp") * 8 + lax.axis_index("tensor")
    bit = bits_of(dev)
    width = teacher_head.shape[1]
    per = teacher_hidden.shape[0]
    dt, ds = teacher_hidden.shape[1], student_hidden.shape[1]

    ids = jnp.stack([target_ids // 256, target_ids % 256], axis=1).astype(BF16)
    own = jnp.concatenate([teacher_hidden, student_hidden, jnp.pad(ids, ((0, 0), (0, 126)))], axis=1)

    place, spots = [], []
    for call in CALLS:
        for i, late in call:
            first, n, slices, order = PARTS[i]
            half = n << (len(order) - 1)
            row = np.arange(late * half, (late + 1) * half, GROUP)
            rel = {d: (row // n >> k & 1).astype(np.int32) for k, d in enumerate(order)}
            if "Xa" in rel:
                a, b = rel["Xa"], rel["Xb"]
                rel["X1"] = a * (1 - bit["C"]) + b * bit["C"]
                rel["X0"] = b * (1 - bit["C"]) + a * bit["C"]
            (d,) = slices
            inner = first + (rel[d] ^ bit[d]) * n + (row % n).astype(np.int32)
            near = (rel["X1"] * 4 + rel["Yb"] * 2 + rel["Ya"]) * per
            fixed = ((rel["X1"] ^ bit["X1"]) * 4 + (rel["Yb"] ^ bit["Yb"]) * 2 + (rel["Ya"] ^ bit["Ya"])) * per
            place.append((near + inner) // GROUP)
            spots.append((fixed + inner) // GROUP)
    size = [sum(p.shape[0] for p in place[sum(map(len, CALLS[:k])) :][: len(call)]) for k, call in enumerate(CALLS)]
    place, spots = jnp.concatenate(place).astype(jnp.int32), jnp.concatenate(spots).astype(jnp.int32)
    spots_of = [spots[sum(size[:k]) : sum(size[: k + 1])] for k in range(len(CALLS))]
    turn = []
    for x0 in (0, 1):
        for zb in (0, 1):
            for za in (0, 1):
                xl = bit["X0"] ^ x0 ^ bit["X1"]
                z = z_of({"C": bit["C"], "Zb": bit["Zb"] ^ zb, "Za": bit["Za"] ^ za})
                turn.append(jnp.int32(xl * 4 + z))
    turn = jnp.stack(turn)
    firsts = jnp.stack([dev * width, (dev ^ 8) * width]).astype(jnp.int32)

    state = []
    for first, n, slices, _ in PARTS:
        index = 0
        for d in slices:
            index = index * 2 + bit[d]
        state.append([lax.dynamic_slice_in_dim(own, first + index * n, n, 0) if slices else own[first : first + n]])
    student_other, teacher_other = swap(student_head, "C"), swap(teacher_head, "C")
    for step in range(3):
        if step == 2:
            state, student_other, teacher_other = lax.optimization_barrier((state, student_other, teacher_other))
        elif step == 1:
            tables = (place, spots, spots_of, turn, firsts)
            state, tables = lax.optimization_barrier((state, tables))
            place, spots, spots_of, turn, firsts = tables
        dims = [order[step] for *_, order in PARTS]
        for d in sorted(set(dims)):
            members = [i for i, other in enumerate(dims) if other == d]
            mine = [state[i][0] for i in members]
            got = swap(jnp.concatenate(mine, axis=0) if len(mine) > 1 else mine[0], d)
            at = 0
            for i, x in zip(members, mine):
                state[i] = [x, got[at : at + x.shape[0]] if len(mine) > 1 else got]
                at += x.shape[0]
                if step < 2 or i not in EARLY:
                    state[i] = [jnp.concatenate(state[i], axis=0)]
    state = [(early, [swap(x, order[3]) for x in early]) for early, (*_, order) in zip(state, PARTS)]

    heads = (teacher_head, teacher_other, student_head, student_other)
    expos, rows, rows_other, side, at = [], [], [], (), 0
    for call, spots_here in zip(CALLS, spots_of):
        chunks = [x for i, late in call for x in state[i][late]]
        n = sum(x.shape[0] for x in chunks)
        e_t, e_s, r, *side = logits(chunks, spots_here, firsts, heads, per * 8, side)
        expos += [e_t, e_s]
        rows.append(r)
        at += n
    rows_other = [swap(r, "C") for r in rows]
    stats, targets = side
    local = stats
    for d in STAT_ORDER:
        stats = merge(stats, swap(stats, d))

    total, wide, cut = at, ds // 8, per // 2
    vmem = pl.BlockSpec(memory_space=pltpu.VMEM)
    smem = pl.BlockSpec(memory_space=pltpu.SMEM)
    shape = jax.ShapeDtypeStruct
    u, v = (2, 2, 2, 2, 2, cut, wide), (2, 2, 2, 2, 2, per - cut, wide)
    outs = [((total, width), BF16)] * 2 + [(u, F32), (u, BF16), (v, F32), (v, BF16)]
    far = pl.BlockSpec(memory_space=pl.ANY)
    g_own, g_other, u_keep, u_send, v_keep, v_send = pl.pallas_call(
        grad_kernel,
        out_shape=[shape(*o) for o in outs],
        in_specs=[smem] * 4 + [vmem] * 3 + [far] * (len(expos) + 2),
        out_specs=[far] * 6,
        scratch_shapes=[pltpu.VMEM(*o) for o in outs]
        + [
            pltpu.VMEM((total, 2 * width), F32),
            pltpu.VMEM((total, 2 * width), BF16),
            pltpu.VMEM((total, 128), F32),
            pltpu.VMEM((2, total, 2 * width), F32),
            pltpu.VMEM((ds, 2 * width), BF16),
            pltpu.SemaphoreType.DMA((len(expos) + 4 + 3 * 4,)),
        ],
        compiler_params=pltpu.CompilerParams(vmem_limit_bytes=56 * 2**20),
        name="grad",
    )(
        place, spots, turn, firsts, stats, local, targets, *expos, student_head, student_other
    )
    head_grad = head_gradient(rows + rows_other, g_own, swap(g_other, "C"))

    streams = [
        [u_keep, u_send, ("Zb", "Yb", "Za", "Ya", "X1", "X0")],
        [v_keep, v_send, ("Yb", "Zb", "Ya", "Za", "X0", "X1")],
    ]
    for step in range(6):
        back = [swap(s[1], s[2][step]) for s in streams]
        if step == 0:
            back[0], back[1], head_grad = lax.optimization_barrier((back[0], back[1], head_grad))
        for s, got in zip(streams, back):
            new = s[0] + got.astype(F32)
            if step == 5:
                s[0] = new
                continue
            s[0], send = new[0], new[1]
            s[1] = send.astype(BF16) if step + 1 < NARROW_STEPS else send
    input_grad = jnp.concatenate([s[0] for s in streams], axis=0)
    return (head_grad, input_grad)


def solution(mesh):
    placed = (
        P("dp", None),
        P("dp", None),
        P("dp"),
        P(None, ("dp", "tensor")),
        P(None, ("dp", "tensor")),
    )
    return jax.shard_map(
        body,
        mesh=mesh,
        in_specs=placed,
        out_specs=(P(None, ("dp", "tensor")), P("dp", "tensor")),
        check_vma=False,
    )
```

```python
import functools

import jax
import jax.numpy as jnp
import numpy as np
from jax import lax
from jax.experimental import pallas as pl
from jax.experimental.pallas import tpu as pltpu
from jax.sharding import PartitionSpec as P

VOCAB = 64128
F32, BF16 = jnp.float32, jnp.bfloat16
AXES = ("dp", "tensor")

PARTS = (
    (0, 24, ("Zb",), ("X1", "Ya", "Zb", "Yb")),
    (48, 24, ("X0",), ("Yb", "Ya", "Xa", "Xb")),
    (96, 16, ("Za",), ("Yb", "X1", "Ya", "Za")),
)
CALLS = (((0, 0), (1, 0), (2, 0)), ((2, 1),), ((0, 1), (1, 1)))
STAT_ORDER = ("Ya", "Za", "X0", "X1", "Zb", "Yb")
NARROW_STEPS = 4
GROUP = 8
TALL = 32
SLAB = 512


def bits_of(dev):
    dp, tensor = dev // 8, dev % 8
    xh, y, core = dp // 8, (dp // 2) % 4, dp % 2
    xl, z = tensor // 4, tensor % 4
    gx, gy, gz = xh * 2 + (xh ^ xl), y ^ (y // 2), z ^ (z // 2)
    pick = lambda g, second: (g // 2) * second + (g % 2) * (1 - second)
    return {
        "X1": xh, "X0": xh ^ xl,
        "Xa": pick(gx, 1 - core), "Xb": pick(gx, core),
        "Ya": pick(gy, core), "Yb": pick(gy, 1 - core),
        "Za": pick(gz, core), "Zb": pick(gz, 1 - core),
        "C": core,
    }


def z_of(bits):
    core = bits["C"]
    high = bits["Zb"] * (1 - core) + bits["Za"] * core
    low = bits["Za"] * (1 - core) + bits["Zb"] * core
    return high * 2 + (high ^ low)


@functools.cache
def pairs(dim):
    if dim == "C":
        return [(d, d ^ 8) for d in range(128)]
    basis = ("X1", "X0", "Ya", "Yb", "Za", "Zb", "C")
    key = lambda b: tuple(b[k] for k in basis)
    table = {key(bits_of(d)): d for d in range(128)}
    out = []
    for d in range(128):
        b = bits_of(d)
        real = dim
        if dim in ("Xa", "Xb"):
            real = "X1" if (dim == "Xa") == (b["C"] == 0) else "X0"
        out.append((d, table[key(dict(b, **{real: 1 - b[real]}))]))
    return out


def swap(x, dim):
    return lax.ppermute(x, AXES, pairs(dim))


def logits_kernel(counts, last, place, first, *refs):
    n = len(counts)
    x_refs = refs[:n]
    heads = refs[n : n + 4]
    earlier = refs[n + 4 : n + 6]
    e_t, e_s, rows_out, stats, targets, canon, lines, x, w_t, w_s, z_t, z_s, sems = refs[n + 4 + 2 * last :]
    dt, ds, width = w_t.shape[0], w_s.shape[0], heads[0].shape[1]
    total = sum(counts)
    copies = []

    def copy(src, dst):
        copies.append(pltpu.make_async_copy(src, dst, sems.at[len(copies)]))
        copies[-1].start()
        return copies[-1]

    def rows_in(cols):
        out, at = [], 0
        for ref, count in zip(x_refs, counts):
            out.append(copy(ref.at[:, cols], x.at[pl.ds(at, count), cols]))
            at += count
        return out

    def slabs_in(own, other, w, depth):
        return [
            [
                copy(head.at[pl.ds(lo, SLAB), :], w.at[pl.ds(lo, SLAB), pl.ds(half * width, width)])
                for half, head in enumerate((own, other))
            ]
            for lo in range(0, depth, SLAB)
        ]

    x_s = rows_in(pl.ds(dt, x.shape[1] - dt))
    in_s = slabs_in(heads[2], heads[3], w_s, ds)
    x_t = rows_in(pl.ds(0, dt))
    in_t = slabs_in(heads[0], heads[1], w_t, dt)
    outs = []
    canon[...] = jnp.zeros_like(canon)
    lane = lax.broadcasted_iota(jnp.int32, (TALL, 128), 1)
    lane_width = lax.broadcasted_iota(jnp.int32, (1, width), 1)
    real = jnp.concatenate([first[half] + lane_width < VOCAB for half in (0, 1)], axis=1)

    def products(arrived, lo, w, z):
        for k, slab in enumerate(arrived):
            for c in slab:
                c.wait()
            for left in range(0, 2 * width, 256):
                r = jnp.dot(
                    x[:, lo + k * SLAB : lo + (k + 1) * SLAB],
                    w[k * SLAB : (k + 1) * SLAB, left : left + 256],
                    preferred_element_type=F32,
                )
                z[:, left : left + 256] = r if k == 0 else z[:, left : left + 256] + r

    def exponentials(z, rows):
        value = jnp.where(real, z[rows, :], F32(-1e30))
        top = jnp.max(value, axis=1, keepdims=True)
        e = jnp.exp(value - top)
        z[rows, :] = e
        return top, jnp.sum(e, axis=1, keepdims=True)

    for c in x_s:
        c.wait()
    outs.append(copy(x.at[:, pl.ds(dt, ds)], rows_out))
    products(in_s, dt, w_s, z_s)
    for lo in range(0, total, TALL):
        rows = slice(lo, lo + TALL)
        digits = x[rows, dt + ds :].astype(F32)
        m_s, n_s = exponentials(z_s, rows)
        line = jnp.where(lane == 1, m_s, 0.0)
        line = jnp.where(lane == 3, n_s, line)
        lines[rows, :] = jnp.where(lane == 4, digits[:, 0:1] * 256.0 + digits[:, 1:2], line)
    outs.append(copy(z_s, e_s))
    for c in x_t:
        c.wait()
    products(in_t, 0, w_t, z_t)
    for lo in range(0, total, TALL):
        rows = slice(lo, lo + TALL)
        m_t, n_t = exponentials(z_t, rows)
        line = jnp.where(lane == 0, m_t, lines[rows, :])
        line = jnp.where(lane == 2, n_t, line)
        for k in range(0, TALL, GROUP):
            spot = pl.multiple_of(place[(lo + k) // GROUP] * GROUP, GROUP)
            canon[pl.ds(spot, GROUP), :] = line[k : k + GROUP, :]
        if (lo + TALL) % 128 == 0:
            part = pl.ds(lo + TALL - 128, 128)
            outs.append(copy(z_t.at[part, :], e_t.at[part, :]))
    for i in range(8):
        across = canon[i * 128 : (i + 1) * 128, :].T
        for j in range(5):
            out, old = (stats.at[j], earlier[0].at[j] if last else None) if j < 4 else (targets, earlier[1] if last else None)
            value = across[j : j + 1, :]
            out[i : i + 1, :] = value + old[i : i + 1, :] if last else value
    for c in outs:
        c.wait()


def logits(chunks, place, firsts, heads, rows, earlier):
    counts = tuple(x.shape[0] for x in chunks)
    total = sum(counts)
    dt, (ds, width) = heads[0].shape[0], heads[2].shape
    shape = jax.ShapeDtypeStruct
    smem, vmem, far = (pl.BlockSpec(memory_space=m) for m in (pltpu.SMEM, pltpu.VMEM, pl.ANY))
    n_copies = 2 * len(chunks) + 2 * (dt + ds) // SLAB + 2 + total // 128
    return pl.pallas_call(
        functools.partial(logits_kernel, counts, bool(earlier)),
        out_shape=[
            shape((total, 2 * width), F32), shape((total, 2 * width), F32), shape((total, ds), BF16),
            shape((4, 8, 128), F32), shape((8, 128), F32),
        ],
        in_specs=[smem] * 2 + [far] * (len(chunks) + 4) + [vmem] * len(earlier),
        out_specs=[far] * 3 + [vmem] * 2,
        scratch_shapes=[
            pltpu.VMEM((rows, 128), F32),
            pltpu.VMEM((total, 128), F32),
            pltpu.VMEM((total, chunks[0].shape[1]), BF16),
            pltpu.VMEM((dt, 2 * width), BF16),
            pltpu.VMEM((ds, 2 * width), BF16),
            pltpu.VMEM((total, 2 * width), F32),
            pltpu.VMEM((total, 2 * width), F32),
            pltpu.SemaphoreType.DMA((n_copies,)),
        ],
        compiler_params=pltpu.CompilerParams(vmem_limit_bytes=56 * 2**20),
        cost_estimate=pl.CostEstimate(flops=10**11, bytes_accessed=0, transcendentals=0),
        name="logits",
    )(place, firsts, *chunks, *heads, *earlier)


def merge(mine, got):
    top = jnp.maximum(mine[:2], got[:2])
    sums = mine[2:] * jnp.exp(mine[:2] - top) + got[2:] * jnp.exp(got[:2] - top)
    return jnp.concatenate([top, sums], axis=0)


def grad_kernel(place, spots, turn, first, stats, local, targets, *refs):
    n = 2 * len(CALLS)
    e_hbm, heads, outs = refs[:n], refs[n : n + 2], refs[n + 2 : n + 8]
    g_own, g_other, u_keep, u_send, v_keep, v_send = refs[n + 8 : n + 14]
    canon, block, scales, e_all, w, sems = refs[n + 14 :]
    width = heads[0].shape[1]
    total = canon.shape[0]
    copies = []

    def copy(src, dst):
        copies.append(pltpu.make_async_copy(src, dst, sems.at[len(copies)]))
        copies[-1].start()
        return copies[-1]

    in_e, edge = [], [0]
    for i, e in enumerate(e_hbm):
        in_e.append(copy(e, e_all.at[i % 2, pl.ds(edge[-1], e.shape[0]), :]))
        if i % 2:
            edge.append(edge[-1] + e.shape[0])
    in_w = [copy(head, w.at[:, pl.ds(i * width, width)]) for i, head in enumerate(heads)]
    row = lax.broadcasted_iota(jnp.int32, (128, 128), 0)
    for i in range(8):
        tile = jnp.where(row == 2, targets[i : i + 1, :], 0.0)
        for j in (0, 1):
            scale = jnp.exp(local[j, i : i + 1, :] - stats[j, i : i + 1, :]) / stats[2 + j, i : i + 1, :]
            tile = jnp.where(row == j, (1.0 + j) * scale, tile)
        scales[i * 128 : (i + 1) * 128, :] = tile.T

    for call in range(len(CALLS)):
        in_e[2 * call].wait()
        in_e[2 * call + 1].wait()

        def rows16(i, _):
            here = pl.multiple_of(i * 16, 16)
            groups = [2 * i + k for k in (0, 1)]
            there = [pl.multiple_of(place[g] * GROUP, GROUP) for g in groups]
            s = jnp.concatenate(
                [scales[pl.ds(pl.multiple_of(spots[g] * GROUP, GROUP), GROUP), :] for g in groups], axis=0
            )
            target = s[:, 2:3].astype(jnp.int32)
            for half, out in ((0, g_own), (1, g_other)):
                cols = slice(half * width, (half + 1) * width)
                column = first[half] + lax.broadcasted_iota(jnp.int32, (16, width), 1)
                g = e_all[1, pl.ds(here, 16), cols] * s[:, 1:2] - e_all[0, pl.ds(here, 16), cols] * s[:, 0:1]
                g = jnp.where(target == column, g - 1.0, g)
                out[pl.ds(here, 16), :] = g.astype(BF16)
                for k in (0, 1):
                    canon[pl.ds(there[k], GROUP), cols] = g[k * GROUP : (k + 1) * GROUP, :]
            return 0

        lax.fori_loop(edge[call] // 16, edge[call + 1] // 16, rows16, 0, unroll=4)
    waits = [copy(g_own, outs[0]), copy(g_other, outs[1])]
    block[...] = canon[...].astype(BF16)
    for c in in_w:
        c.wait()

    wide, cut = u_keep.shape[-1], u_keep.shape[-2]
    for zb in (1, 0):
        for za in (1, 0):
            for x0 in (1, 0):
                where = pl.multiple_of(turn[x0 * 4 + zb * 2 + za] * wide, wide)
                r = lax.dot_general(
                    block[...], w[pl.ds(where, wide), :], (((1,), (1,)), ((), ())), preferred_element_type=F32
                ).reshape(2, 2, 2, total // 8, wide)
                for h in (0, 1):
                    x = x0 ^ h
                    for ya in (0, 1):
                        for yb in (0, 1):
                            low = r[h, yb, ya, :cut]
                            if zb == 0:
                                u_keep[yb, za, ya, h, x] = low
                            else:
                                u_send[yb, za, ya, h, x] = low.astype(BF16)
                        v_keep[zb, ya, za, x, h] = r[h, 0, ya, cut:]
                        v_send[zb, ya, za, x, h] = r[h, 1, ya, cut:].astype(BF16)
            pair = (u_send, outs[3]) if zb else (u_keep, outs[2])
            waits.append(copy(*(ref.at[:, za] for ref in pair)))
            for pair in ((v_keep, outs[4]), (v_send, outs[5])):
                waits.append(copy(*(ref.at[zb, :, za] for ref in pair)))
    for c in waits:
        c.wait()


def head_kernel(*refs):
    *rows, g, g_other, out = refs
    total, at = None, 0
    for r in rows:
        n = r.shape[0]
        lo = at % g.shape[0]
        part = (g if at < g.shape[0] else g_other)[lo : lo + n, :]
        product = lax.dot_general(r[...], part, (((0,), (0,)), ((), ())), preferred_element_type=F32)
        total = product if total is None else total + product
        at += n
    out[...] = total


def head_gradient(rows, g, g_other):
    ds, (total, width) = rows[0].shape[1], g.shape
    tile = 256
    whole = pl.BlockSpec(g.shape, lambda i: (0, 0))
    return pl.pallas_call(
        head_kernel,
        grid=(ds // tile,),
        out_shape=jax.ShapeDtypeStruct((ds, width), F32),
        in_specs=[pl.BlockSpec((r.shape[0], tile), lambda i: (0, i)) for r in rows] + [whole] * 2,
        out_specs=pl.BlockSpec((tile, width), lambda i: (i, 0)),
        compiler_params=pltpu.CompilerParams(vmem_limit_bytes=32 * 2**20),
        cost_estimate=pl.CostEstimate(flops=10**11, bytes_accessed=0, transcendentals=0),
        name="head",
    )(*rows, g, g_other)


def body(teacher_hidden, student_hidden, target_ids, teacher_head, student_head):
    dev = lax.axis_index("dp") * 8 + lax.axis_index("tensor")
    bit = bits_of(dev)
    width = teacher_head.shape[1]
    per = teacher_hidden.shape[0]
    dt, ds = teacher_hidden.shape[1], student_hidden.shape[1]

    ids = jnp.stack([target_ids // 256, target_ids % 256], axis=1).astype(BF16)
    own = jnp.concatenate([teacher_hidden, student_hidden, jnp.pad(ids, ((0, 0), (0, 126)))], axis=1)

    place, spots = [], []
    for call in CALLS:
        for i, late in call:
            first, n, slices, order = PARTS[i]
            half = n << (len(order) - 1)
            row = np.arange(late * half, (late + 1) * half, GROUP)
            rel = {d: (row // n >> k & 1).astype(np.int32) for k, d in enumerate(order)}
            if "Xa" in rel:
                a, b = rel["Xa"], rel["Xb"]
                rel["X1"] = a * (1 - bit["C"]) + b * bit["C"]
                rel["X0"] = b * (1 - bit["C"]) + a * bit["C"]
            (d,) = slices
            inner = first + (rel[d] ^ bit[d]) * n + (row % n).astype(np.int32)
            near = (rel["X1"] * 4 + rel["Yb"] * 2 + rel["Ya"]) * per
            fixed = ((rel["X1"] ^ bit["X1"]) * 4 + (rel["Yb"] ^ bit["Yb"]) * 2 + (rel["Ya"] ^ bit["Ya"])) * per
            place.append((near + inner) // GROUP)
            spots.append((fixed + inner) // GROUP)
    size = [sum(p.shape[0] for p in place[sum(map(len, CALLS[:k])) :][: len(call)]) for k, call in enumerate(CALLS)]
    place, spots = jnp.concatenate(place).astype(jnp.int32), jnp.concatenate(spots).astype(jnp.int32)
    spots_of = [spots[sum(size[:k]) : sum(size[: k + 1])] for k in range(len(CALLS))]
    turn = []
    for x0 in (0, 1):
        for zb in (0, 1):
            for za in (0, 1):
                xl = bit["X0"] ^ x0 ^ bit["X1"]
                z = z_of({"C": bit["C"], "Zb": bit["Zb"] ^ zb, "Za": bit["Za"] ^ za})
                turn.append(jnp.int32(xl * 4 + z))
    turn = jnp.stack(turn)
    firsts = jnp.stack([dev * width, (dev ^ 8) * width]).astype(jnp.int32)

    state = []
    for first, n, slices, _ in PARTS:
        index = 0
        for d in slices:
            index = index * 2 + bit[d]
        state.append([lax.dynamic_slice_in_dim(own, first + index * n, n, 0) if slices else own[first : first + n]])
    student_other, teacher_other = swap(student_head, "C"), swap(teacher_head, "C")
    for step in range(4):
        if step == 2:
            state, student_other, teacher_other = lax.optimization_barrier((state, student_other, teacher_other))
        elif step == 1:
            tables = (place, spots, spots_of, turn, firsts)
            state, tables = lax.optimization_barrier((state, tables))
            place, spots, spots_of, turn, firsts = tables
        elif step:
            state = lax.optimization_barrier(state)
        dims = [order[step] for *_, order in PARTS]
        for d in sorted(set(dims)):
            members = [i for i, other in enumerate(dims) if other == d]
            mine = [state[i][0] for i in members]
            got = swap(jnp.concatenate(mine, axis=0) if len(mine) > 1 else mine[0], d)
            at = 0
            for i, x in zip(members, mine):
                state[i] = [x, got[at : at + x.shape[0]] if len(mine) > 1 else got]
                at += x.shape[0]
                if step < 3:
                    state[i] = [jnp.concatenate(state[i], axis=0)]

    heads = (teacher_head, teacher_other, student_head, student_other)
    expos, rows, rows_other, side, at = [], [], [], (), 0
    for call, spots_here in zip(CALLS, spots_of):
        chunks = [state[i][late] for i, late in call]
        n = sum(x.shape[0] for x in chunks)
        e_t, e_s, r, *side = logits(chunks, spots_here, firsts, heads, per * 8, side)
        expos += [e_t, e_s]
        rows.append(r)
        at += n
    rows_other = [swap(r, "C") for r in rows]
    stats, targets = side
    local = stats
    for d in STAT_ORDER:
        stats = merge(stats, swap(stats, d))

    total, wide, cut = at, ds // 8, per // 2
    vmem = pl.BlockSpec(memory_space=pltpu.VMEM)
    smem = pl.BlockSpec(memory_space=pltpu.SMEM)
    shape = jax.ShapeDtypeStruct
    u, v = (2, 2, 2, 2, 2, cut, wide), (2, 2, 2, 2, 2, per - cut, wide)
    outs = [((total, width), BF16)] * 2 + [(u, F32), (u, BF16), (v, F32), (v, BF16)]
    far = pl.BlockSpec(memory_space=pl.ANY)
    g_own, g_other, u_keep, u_send, v_keep, v_send = pl.pallas_call(
        grad_kernel,
        out_shape=[shape(*o) for o in outs],
        in_specs=[smem] * 4 + [vmem] * 3 + [far] * (len(expos) + 2),
        out_specs=[far] * 6,
        scratch_shapes=[pltpu.VMEM(*o) for o in outs]
        + [
            pltpu.VMEM((total, 2 * width), F32),
            pltpu.VMEM((total, 2 * width), BF16),
            pltpu.VMEM((total, 128), F32),
            pltpu.VMEM((2, total, 2 * width), F32),
            pltpu.VMEM((ds, 2 * width), BF16),
            pltpu.SemaphoreType.DMA((len(expos) + 4 + 3 * 4,)),
        ],
        compiler_params=pltpu.CompilerParams(vmem_limit_bytes=56 * 2**20),
        name="grad",
    )(
        place, spots, turn, firsts, stats, local, targets, *expos, student_head, student_other
    )
    head_grad = head_gradient(rows + rows_other, g_own, swap(g_other, "C"))

    streams = [
        [u_keep, u_send, ("Zb", "Yb", "Za", "Ya", "X1", "X0")],
        [v_keep, v_send, ("Yb", "Zb", "Ya", "Za", "X0", "X1")],
    ]
    for step in range(6):
        back = [swap(s[1], s[2][step]) for s in streams]
        if step == 0:
            back[0], back[1], head_grad = lax.optimization_barrier((back[0], back[1], head_grad))
        for s, got in zip(streams, back):
            new = s[0] + got.astype(F32)
            if step == 5:
                s[0] = new
                continue
            s[0], send = new[0], new[1]
            s[1] = send.astype(BF16) if step + 1 < NARROW_STEPS else send
    input_grad = jnp.concatenate([s[0] for s in streams], axis=0)
    return (head_grad, input_grad)


def solution(mesh):
    placed = (
        P("dp", None),
        P("dp", None),
        P("dp"),
        P(None, ("dp", "tensor")),
        P(None, ("dp", "tensor")),
    )
    return jax.shard_map(
        body,
        mesh=mesh,
        in_specs=placed,
        out_specs=(P(None, ("dp", "tensor")), P("dp", "tensor")),
        check_vma=False,
    )
```
